256 devices in a mesh: scan: 8 (over x, core), brick: 32 (over z, y).
Axes of the slice: x: 4, y: 4, z: 8, core: 2. Of those that a mesh axis runs over, the one named last changes fastest.
Arguments:
- features: bfloat16 [8, 32, 64, 4096], P('scan', 'brick'), may hold values from -6 to 6
- cotangent: bfloat16 [8, 32, 64, 4096], P('scan', 'brick'), may hold values from -6 to 6
- weight: bfloat16 [27, 64, 64], replicated, may hold values from -0.15625 to 0.15625
- neighbours: int32 [8, 32, 27], P('scan', 'brick'), may hold values from -1 to 31, as said below
- occupancy: int32 [8, 32, 4096], P('scan', 'brick'), may hold values 0 or 1
Outputs:
- output: bfloat16 [8, 32, 64, 4096], P('scan', 'brick')
- grad_input: bfloat16 [8, 32, 64, 4096], P('scan', 'brick')
- grad_weight: float32 [27, 64, 64], replicated
The draws below stay inside these ranges and needn't reach their ends.
Inputs may be any that keep to these rules, and one draw needn't show every extreme that they name: `neighbours`: entry k = 9 (dz + 1) + 3 (dy + 1) + (dx + 1) of brick g names the occupied brick of the same scan at brick offset (dz, dy, dx), or -1; entry 13 is g. Bricks g lie in layer g // 1 of brick positions, so a neighbour at offset dz is one of the bricks of layer g + dz. The relation is symmetric.
All inputs are finite; a program needn't handle non-finite values. No bound on the sum of `occupancy` on one device may be relied on, other than what follows from the above.
Results may differ from the reference program's by a relative error of at most 0.001.
Values may be sent and summed in bfloat16 or wider, within the bound.
A program may use at most 256 MiB of HBM per device.

```python
import jax
import jax.numpy as jnp
from jax import lax

C = 64
BS = 16
GRIDW = 4
BD = 1
NB = 32
V = 4096
N_SCAN = 8
N_BRICK = 32


def draw_neighbours(key, part):
    key = jax.random.fold_in(key, 7)
    cell_total = GRIDW * GRIDW

    def one_scan(scan_key):
        layer_keys = jax.random.split(scan_key, N_BRICK)
        orders = jax.vmap(lambda k: jax.random.permutation(k, cell_total))(layer_keys)
        chosen = orders[:, :BD].reshape(-1).astype(jnp.int32)
        layer_of = (jnp.arange(N_BRICK * BD) // BD).astype(jnp.int32)
        lookup_table = jnp.full((N_BRICK, cell_total), -1, jnp.int32).at[layer_of, chosen].set(jnp.arange(N_BRICK * BD, dtype=jnp.int32))
        row_of = chosen // GRIDW
        col_of = chosen % GRIDW
        columns = []
        for k in range(27):
            layer_at = layer_of + (k // 9 - 1)
            row_at = row_of + (k // 3 % 3 - 1)
            col_at = col_of + (k % 3 - 1)
            inside = (layer_at >= 0) & (layer_at < N_BRICK) & (row_at >= 0) & (row_at < GRIDW) & (col_at >= 0) & (col_at < GRIDW)
            located = lookup_table[jnp.clip(layer_at, 0, N_BRICK - 1), jnp.clip(row_at, 0, GRIDW - 1) * GRIDW + jnp.clip(col_at, 0, GRIDW - 1)]
            columns.append(jnp.where(inside, located, -1))
        return jnp.stack(columns, axis=1).astype(jnp.int32)
    return jax.vmap(one_scan)(jax.random.split(key, N_SCAN))


def touch_ends(result, key, least, high):
    longest = result.shape.index(max(result.shape))
    spots = []
    for shift in (0, 1):
        where = [jax.random.randint(jax.random.fold_in(key, axis), (), 0, length) for axis, length in enumerate(result.shape)]
        where[longest] = (where[longest] + shift) % result.shape[longest]
        spots.append(tuple(where))
    return result.at[spots[0]].set(least).at[spots[1]].set(high)


def block_levels(key, extent, shards, smallest, top_value):
    gain = 1.0
    for dim, parts in shards:
        draws = jax.random.uniform(jax.random.fold_in(jax.random.fold_in(key, 6), dim), (parts,), jnp.float32, smallest / len(shards), top_value / len(shards))
        gain = gain * jnp.repeat(jnp.exp(draws), extent[dim] // parts).reshape((-1,) + (1,) * (len(extent) - 1 - dim))
    return gain


def bell_draw(stream_key, shape, deviation, bound, cuts=(), kind=jnp.bfloat16):
    drawn = jax.random.normal(stream_key, shape, jnp.float32) * deviation
    if len(cuts) > 0:
        drawn = block_levels(stream_key, shape, cuts, -0.22, 0.18) * drawn
    return jnp.clip(drawn, min=-bound, max=bound).astype(kind)


def setup_inputs(seed: int = 0) -> dict:
    splits = jax.random.split(jax.random.key(seed), 6)
    features = bell_draw(splits[0], (N_SCAN, NB, C, V), 1.0, 6.0, ((0, 8), (1, 32)))
    cotangent = bell_draw(splits[1], (N_SCAN, NB, C, V), 1.0, 6.0, ((0, 8), (1, 32)))
    weight = bell_draw(splits[2], (27, C, C), (27 * C) ** -0.5, 0.15625)
    neighbours = draw_neighbours(jax.random.fold_in(splits[5], 71), 0)
    occupancy = touch_ends((jax.random.randint(splits[4], (N_SCAN, NB, V), 0, 2) < 1).astype(jnp.int32), jax.random.fold_in(splits[4], 1), 0, 1)
    return {"features": features, "cotangent": cotangent, "weight": weight, "neighbours": neighbours, "occupancy": occupancy}


def assemble(lower_pool, own_pool, upper_pool, offset_rows, valid_rows):
    layer_parts = []
    for shift_z in (-1, 0, 1):
        source_pool = (lower_pool, own_pool, upper_pool)[shift_z + 1]
        plane_parts = []
        for shift_y in (-1, 0, 1):
            columns = []
            for shift_x in (-1, 0, 1):
                k = 9 * (shift_z + 1) + 3 * (shift_y + 1) + (shift_x + 1)
                y_part = (slice(BS - 1, BS), slice(0, BS), slice(0, 1))[shift_y + 1]
                x_part = (slice(BS - 1, BS), slice(0, BS), slice(0, 1))[shift_x + 1]
                portion = source_pool[:, :, :, y_part, x_part]
                fetched = jnp.take(portion, offset_rows[:, k], axis=0)
                fetched = jnp.where(valid_rows[:, k][:, None, None, None, None], fetched, jnp.zeros_like(fetched))
                columns.append(fetched)
            plane_parts.append(jnp.concatenate(columns, axis=4))
        layer_parts.append(jnp.concatenate(plane_parts, axis=3))
    return jnp.concatenate(layer_parts, axis=2)


def moved_field(padded, k, sign):
    start_z = 1 + sign * (k // 9 - 1)
    start_y = 1 + sign * (k // 3 % 3 - 1)
    start_x = 1 + sign * (k % 3 - 1)
    moved = padded[:, :, start_z:start_z + BS, start_y:start_y + BS, start_x:start_x + BS]
    return moved.reshape(padded.shape[0], padded.shape[1], BS ** 3)


def convolve(padded, kernel, sign):
    summed = jnp.zeros((padded.shape[0], kernel.shape[1], BS ** 3), jnp.float32)
    for k in range(27):
        moved = moved_field(padded, k, sign)
        summed = summed + jnp.einsum("oc,bcv->bov", kernel[k].astype(jnp.float32), moved.astype(jnp.float32))
    return summed


def one_scan(inputs, weight):
    feats, grads, nbr, occ = inputs
    voxel_mask = occ.astype(jnp.bfloat16)[:, None, :]
    valid_rows = nbr >= 0
    offset_rows = jnp.maximum(nbr, 0).astype(jnp.int32)
    live_feat = feats * voxel_mask
    live_cube = live_feat.reshape(NB, C, BS, BS, BS)
    padded = assemble(live_cube[:, :, BS - 1:BS], live_cube, live_cube[:, :, 0:1], offset_rows, valid_rows)
    output = (convolve(padded, weight, 1) * voxel_mask.astype(jnp.float32)).astype(jnp.bfloat16)
    upstream = grads * voxel_mask
    up_cube = upstream.reshape(NB, C, BS, BS, BS)
    up_padded = assemble(up_cube[:, :, BS - 1:BS], up_cube, up_cube[:, :, 0:1], offset_rows, valid_rows)
    flipped = jnp.transpose(weight, (0, 2, 1))
    grad_input = (convolve(up_padded, flipped, -1) * voxel_mask.astype(jnp.float32)).astype(jnp.bfloat16)
    terms = []
    for k in range(27):
        moved = moved_field(padded, k, 1)
        terms.append(jnp.einsum("bov,bcv->oc", upstream.astype(jnp.float32), moved.astype(jnp.float32)))
    return output, grad_input, jnp.stack(terms)


def reference(features, cotangent, weight, neighbours, occupancy):
    output, grad_input, weight_terms = lax.map(lambda inputs: one_scan(inputs, weight), (features, cotangent, neighbours, occupancy))
    return output, grad_input, jnp.sum(weight_terms, axis=0)
```

```python
import jax
import jax.numpy as jnp
from jax import lax
from jax.experimental import pallas as pl
from jax.experimental.pallas import tpu as pltpu
from jax.sharding import PartitionSpec as P

C = 64
BS = 16
PLANE = BS * BS
V = BS * PLANE
EXT = (BS + 2) * PLANE
TAPS = 9
BF = jnp.bfloat16
F32 = jnp.float32
MESH = pl.DeviceIdType.MESH
N_CORE, N_X, N_Y, N_Z = 2, 4, 4, 8
N_BRICK = N_Y * N_Z
N_XY = N_X * N_Y


def spread(plane, x_iota):
    left = jnp.where(x_iota == 0, pltpu.roll(plane, PLANE - 15, 1), pltpu.roll(plane, 1, 1))
    right = jnp.where(x_iota == BS - 1, pltpu.roll(plane, 15, 1), pltpu.roll(plane, PLANE - 1, 1))
    shifted = []
    for dy in (-1, 0, 1):
        for base in (left, plane, right):
            shifted.append(base if dy == 0 else pltpu.roll(base, (-dy * BS) % PLANE, 1))
    return shifted


def kernel(
    feat_hbm, cot_hbm, w_ref, nb_ref, occ_ref,
    out_hbm, gin_hbm, gw_ref,
    feat_v, cot_v, out_v, gin_v, mask_v, s9f, s9u, u3, wf, wb,
    halo_send, halo_recv, part, pair_recv, half, xy_recv, own, z_recv, total, final,
    in_sem, out_sem, halo_ssem, halo_rsem, ar_ssem, ar_rsem,
):
    scan = lax.axis_index("scan")
    brick = lax.axis_index("brick")
    cx, cc = scan // N_CORE, scan % N_CORE
    cz, cy = brick // N_Y, brick % N_Y
    xy = cx * N_Y + cy
    up_dev = (scan, lax.rem(brick + 1, N_BRICK))
    down_dev = (scan, lax.rem(brick + N_BRICK - 1, N_BRICK))
    pair_dev = (cx * N_CORE + 1 - cc, brick)

    def xy_peer(j):
        i = lax.rem(xy + j, N_XY)
        return i, ((i // N_Y) * N_CORE + cc, cz * N_Y + lax.rem(i, N_Y))

    def z_peer(j):
        return (scan, lax.rem(cz + j, N_Z) * N_Y + cy)

    feat_in = pltpu.make_async_copy(feat_hbm, feat_v, in_sem.at[0])
    cot_in = pltpu.make_async_copy(cot_hbm, cot_v, in_sem.at[1])
    feat_in.start()
    cot_in.start()

    barrier = pltpu.get_barrier_semaphore()
    signals = 0
    for dev in [up_dev, down_dev, pair_dev]:
        pl.semaphore_signal(barrier, inc=1, device_id=dev, device_id_type=MESH)
        signals += 1
    for j in range(1, N_XY):
        pl.semaphore_signal(barrier, inc=1, device_id=xy_peer(j)[1], device_id_type=MESH)
        signals += 1
    for j in range(1, N_Z):
        pl.semaphore_signal(barrier, inc=1, device_id=z_peer(j), device_id_type=MESH)
        signals += 1

    lane = lax.broadcasted_iota(jnp.int32, (C, PLANE), 1)
    x_iota = lane % BS
    y_iota = lane // BS
    for layer in range(3):
        flag = [jnp.where(nb_ref[0, 9 * layer + k] >= 0, 1.0, 0.0).astype(F32) for k in range(9)]
        for dy in (-1, 0, 1):
            y_out = y_iota == (BS - 1 if dy == 1 else 0 if dy == -1 else -1)
            for dx in (-1, 0, 1):
                x_out = x_iota == (BS - 1 if dx == 1 else 0 if dx == -1 else -1)

                def at(a, b):
                    return flag[3 * (a + 1) + b + 1]

                inner = jnp.where(x_out, at(0, dx), at(0, 0))
                outer = jnp.where(x_out, at(dy, dx), at(dy, 0))
                mask_v[layer, 3 * (dy + 1) + dx + 1] = jnp.where(y_out, outer, inner).astype(BF)

    def occ_at(z):
        return occ_ref[:, pl.ds(z * PLANE, PLANE)].astype(F32)

    feat_in.wait()
    for n, z in enumerate((BS - 1, 0)):
        halo_send[0, n] = (feat_v[:, z * PLANE : (z + 1) * PLANE].astype(F32) * occ_at(z)).astype(BF)
    pl.semaphore_wait(barrier, signals)

    def halo_copy(field, n):
        return pltpu.make_async_remote_copy(
            src_ref=halo_send.at[field, n],
            dst_ref=halo_recv.at[field, n],
            send_sem=halo_ssem.at[field, n],
            recv_sem=halo_rsem.at[field, n],
            device_id=(up_dev, down_dev)[n],
            device_id_type=MESH,
        )

    halos = [[halo_copy(field, n) for n in range(2)] for field in range(2)]
    halos[0][0].start()
    halos[0][1].start()

    def fill(s9, plane, layer, slot):
        lanes = pl.ds(pl.multiple_of(slot * PLANE, PLANE), PLANE)
        for k, moved in enumerate(spread(plane, x_iota)):
            s9[k * C : (k + 1) * C, lanes] = moved.astype(BF) * mask_v[layer, k]

    cot_in.wait()
    for n, z in enumerate((BS - 1, 0)):
        halo_send[1, n] = (cot_v[:, z * PLANE : (z + 1) * PLANE].astype(F32) * occ_at(z)).astype(BF)
    halos[1][0].start()
    halos[1][1].start()

    u3[...] = jnp.zeros_like(u3)

    def own_planes(z, carry):
        z0 = pl.multiple_of(z * PLANE, PLANE)
        occ = occ_ref[:, pl.ds(z0, PLANE)].astype(F32)
        live = feat_v[:, pl.ds(z0, PLANE)].astype(F32) * occ
        fill(s9f, live, 1, z + 1)
        ups = (cot_v[:, pl.ds(z0, PLANE)].astype(F32) * occ).astype(BF)
        for dz in range(3):
            u3[dz * C : (dz + 1) * C, pl.ds(pl.multiple_of((z + dz) * PLANE, PLANE), PLANE)] = ups
        return carry

    lax.fori_loop(0, BS, own_planes, 0)

    halos[0][0].wait_recv()
    halos[0][1].wait_recv()
    fill(s9f, halo_recv[0, 0].astype(F32), 0, 0)
    fill(s9f, halo_recv[0, 1].astype(F32), 2, BS + 1)

    for t in range(3):
        width = min(PLANE, TAPS * C - t * PLANE)
        g = lax.dot_general(
            u3[...], s9f[t * PLANE : t * PLANE + width, :],
            (((1,), (1,)), ((), ())), preferred_element_type=F32,
        )
        for n in range(0, width, 128):
            for r in range(6):
                w = min(128, width - n)
                part[(2 * t + n // 128) * 6 + r, :, 0:w] = g[32 * r : 32 * r + 32, n : n + w]
    part[24:30, :, C:128] = jnp.zeros((6, 32, C), F32)
    part[30:32] = jnp.zeros((2, 32, 128), F32)

    pair = pltpu.make_async_remote_copy(
        src_ref=part.at[pl.ds((1 - cc) * N_XY, N_XY)],
        dst_ref=pair_recv,
        send_sem=ar_ssem.at[0],
        recv_sem=ar_rsem.at[0],
        device_id=pair_dev,
        device_id_type=MESH,
    )
    pair.start()

    for k in range(27):
        dz, j = k // 9, k % 9
        wf[dz * C : (dz + 1) * C, j * C : (j + 1) * C] = w_ref[k]
        wb[dz * C : (dz + 1) * C, j * C : (j + 1) * C] = jnp.transpose(w_ref[26 - k].astype(F32)).astype(BF)

    pair.wait_recv()
    half[...] = part[pl.ds(cc * N_XY, N_XY)] + pair_recv[...]

    def xy_copy(j):
        i, dev = xy_peer(j)
        return pltpu.make_async_remote_copy(
            src_ref=half.at[i],
            dst_ref=xy_recv.at[j],
            send_sem=ar_ssem.at[j],
            recv_sem=ar_rsem.at[j],
            device_id=dev,
            device_id_type=MESH,
        )

    xy_order = [10, 9, 11, 6, 7, 5, 14, 8, 2, 13, 3, 1, 15, 4, 12]
    xy_copies = {j: xy_copy(j) for j in xy_order}
    for j in xy_order:
        xy_copies[j].start()

    def convolve(weights, s9, dst):
        def product(slot):
            return jnp.dot(
                weights[...], s9[:, pl.ds(pl.multiple_of(slot * PLANE, PLANE), PLANE)],
                preferred_element_type=F32,
            )

        first = product(0)
        second = product(1)

        def step(z, carry):
            low, mid = carry
            r = product(z + 2)
            z0 = pl.multiple_of(z * PLANE, PLANE)
            occ = occ_ref[:, pl.ds(z0, PLANE)].astype(F32)
            dst[:, pl.ds(z0, PLANE)] = ((mid + r[2 * C :]) * occ).astype(BF)
            return r[:C], low + r[C : 2 * C]

        lax.fori_loop(0, BS, step, (second[:C], first[:C] + second[C : 2 * C]))

    convolve(wf, s9f, out_v)
    out_copy = pltpu.make_async_copy(out_v, out_hbm, out_sem.at[0])
    out_copy.start()

    for j in xy_order:
        xy_copies[j].wait_recv()
    own[...] = half[xy]
    for j in range(1, N_XY):
        own[...] += xy_recv[j]

    def z_copy(j):
        return pltpu.make_async_remote_copy(
            src_ref=own,
            dst_ref=z_recv.at[j],
            send_sem=ar_ssem.at[16 + j],
            recv_sem=ar_rsem.at[16 + j],
            device_id=z_peer(j),
            device_id_type=MESH,
        )

    z_order = [4, 3, 5, 2, 6, 1, 7]
    z_copies = {j: z_copy(j) for j in z_order}
    for j in z_order:
        z_copies[j].start()

    halos[1][0].wait_recv()
    halos[1][1].wait_recv()
    fill(s9u, halo_recv[1, 0].astype(F32), 0, 0)
    fill(s9u, halo_recv[1, 1].astype(F32), 2, BS + 1)

    def up_planes(z, carry):
        z0 = pl.multiple_of((z + 1) * PLANE, PLANE)
        fill(s9u, u3[C : 2 * C, pl.ds(z0, PLANE)].astype(F32), 1, z + 1)
        return carry

    lax.fori_loop(0, BS, up_planes, 0)
    convolve(wb, s9u, gin_v)
    gin_copy = pltpu.make_async_copy(gin_v, gin_hbm, out_sem.at[1])
    gin_copy.start()

    for j in z_order:
        z_copies[j].wait_recv()
    z_recv[0] = own[...]
    total[...] = z_recv[cz]
    for s in range(1, N_Z):
        total[...] += z_recv[lax.rem(cz + N_Z - s, N_Z)]

    def back_copy(j):
        i, dev = xy_peer(j)
        return pltpu.make_async_remote_copy(
            src_ref=total,
            dst_ref=final.at[cc * N_XY + xy],
            send_sem=ar_ssem.at[24 + j],
            recv_sem=ar_rsem.at[24 + j],
            device_id=dev,
            device_id_type=MESH,
        )

    back_copies = {j: back_copy(j) for j in xy_order}
    for j in xy_order:
        back_copies[j].start()
    final[cc * N_XY + xy] = total[...]
    for j in xy_order:
        back_copies[j].wait_recv()
    last = pltpu.make_async_remote_copy(
        src_ref=final.at[pl.ds(cc * N_XY, N_XY)],
        dst_ref=final.at[pl.ds(cc * N_XY, N_XY)],
        send_sem=ar_ssem.at[40],
        recv_sem=ar_rsem.at[40],
        device_id=pair_dev,
        device_id_type=MESH,
    )
    last.start()
    last.wait_recv()
    for k in range(27):
        dz, j = k // 9, k % 9
        for h in range(2):
            gw_ref[k, 32 * h : 32 * h + 32, :] = final[(j // 2) * 6 + 2 * dz + h, :, (j % 2) * C : (j % 2 + 1) * C]

    pair.wait_send()
    last.wait_send()
    for j in xy_order:
        xy_copies[j].wait_send()
        back_copies[j].wait_send()
    for j in z_order:
        z_copies[j].wait_send()
    for field in range(2):
        for n in range(2):
            halos[field][n].wait_send()
    out_copy.wait()
    gin_copy.wait()


def local(features, cotangent, weight, neighbours, occupancy):
    vmem = pl.BlockSpec(memory_space=pltpu.VMEM)
    anywhere = pl.BlockSpec(memory_space=pl.ANY)
    field = jax.ShapeDtypeStruct((C, V), BF)
    output, grad_input, grad_weight = pl.pallas_call(
        kernel,
        out_shape=(field, field, jax.ShapeDtypeStruct((27, C, C), F32)),
        in_specs=[anywhere, anywhere, vmem, pl.BlockSpec(memory_space=pltpu.SMEM), vmem],
        out_specs=(anywhere, anywhere, vmem),
        scratch_shapes=[
            pltpu.VMEM((C, V), BF),
            pltpu.VMEM((C, V), BF),
            pltpu.VMEM((C, V), BF),
            pltpu.VMEM((C, V), BF),
            pltpu.VMEM((3, TAPS, C, PLANE), BF),
            pltpu.VMEM((TAPS * C, EXT), BF),
            pltpu.VMEM((TAPS * C, EXT), BF),
            pltpu.VMEM((3 * C, EXT), BF),
            pltpu.VMEM((3 * C, TAPS * C), BF),
            pltpu.VMEM((3 * C, TAPS * C), BF),
            pltpu.VMEM((2, 2, C, PLANE), BF),
            pltpu.VMEM((2, 2, C, PLANE), BF),
            pltpu.VMEM((32, 32, 128), F32),
            pltpu.VMEM((16, 32, 128), F32),
            pltpu.VMEM((16, 32, 128), F32),
            pltpu.VMEM((16, 32, 128), F32),
            pltpu.VMEM((32, 128), F32),
            pltpu.VMEM((8, 32, 128), F32),
            pltpu.VMEM((32, 128), F32),
            pltpu.VMEM((32, 32, 128), F32),
            pltpu.SemaphoreType.DMA((2,)),
            pltpu.SemaphoreType.DMA((2,)),
            pltpu.SemaphoreType.DMA((2, 2)),
            pltpu.SemaphoreType.DMA((2, 2)),
            pltpu.SemaphoreType.DMA((41,)),
            pltpu.SemaphoreType.DMA((41,)),
        ],
        compiler_params=pltpu.CompilerParams(
            collective_id=0, has_side_effects=True, vmem_limit_bytes=50 * 2**20
        ),
    )(
        features.reshape(C, V), cotangent.reshape(C, V), weight,
        neighbours.reshape(1, 27), occupancy.reshape(1, V),
    )
    return output.reshape(1, 1, C, V), grad_input.reshape(1, 1, C, V), grad_weight


def solution(mesh):
    in_specs = (
        P("scan", "brick", None, None),
        P("scan", "brick", None, None),
        P(),
        P("scan", "brick", None),
        P("scan", "brick", None),
    )
    out_specs = (P("scan", "brick", None, None), P("scan", "brick", None, None), P())
    return jax.shard_map(local, mesh=mesh, in_specs=in_specs, out_specs=out_specs, check_vma=False)
```

```python
import jax
import jax.numpy as jnp
from jax import lax
from jax.experimental import pallas as pl
from jax.experimental.pallas import tpu as pltpu
from jax.sharding import PartitionSpec as P

C = 64
BS = 16
PLANE = BS * BS
V = BS * PLANE
EXT = (BS + 2) * PLANE
TAPS = 9
BF = jnp.bfloat16
F32 = jnp.float32
MESH = pl.DeviceIdType.MESH
N_CORE, N_X, N_Y, N_Z = 2, 4, 4, 8
N_BRICK = N_Y * N_Z
N_XY = N_X * N_Y


def spread(plane, x_iota):
    left = jnp.where(x_iota == 0, pltpu.roll(plane, PLANE - 15, 1), pltpu.roll(plane, 1, 1))
    right = jnp.where(x_iota == BS - 1, pltpu.roll(plane, 15, 1), pltpu.roll(plane, PLANE - 1, 1))
    shifted = []
    for dy in (-1, 0, 1):
        for base in (left, plane, right):
            shifted.append(base if dy == 0 else pltpu.roll(base, (-dy * BS) % PLANE, 1))
    return shifted


def kernel(
    feat_hbm, cot_hbm, w_hbm, nb_hbm, occ_hbm,
    out_hbm, gin_hbm, gw_hbm,
    feat_v, cot_v, w_ref, nb_ref, occ_ref, out_v, gin_v, products, mask_v, s9f, s9u, u3, wf, wb,
    halo_send, halo_recv, part, pair_recv, half, xy_recv, own, z_recv, total, final,
    in_sem, out_sem, halo_ssem, halo_rsem, ar_ssem, ar_rsem,
):
    scan = lax.axis_index("scan")
    brick = lax.axis_index("brick")
    cx, cc = scan // N_CORE, scan % N_CORE
    cz, cy = brick // N_Y, brick % N_Y
    xy = cx * N_Y + cy
    up_dev = (scan, lax.rem(brick + 1, N_BRICK))
    down_dev = (scan, lax.rem(brick + N_BRICK - 1, N_BRICK))
    pair_dev = (cx * N_CORE + 1 - cc, brick)

    def xy_peer(j):
        i = lax.rem(xy + j, N_XY)
        return i, ((i // N_Y) * N_CORE + cc, cz * N_Y + lax.rem(i, N_Y))

    def z_peer(j):
        return (scan, lax.rem(cz + j, N_Z) * N_Y + cy)

    feat_in = pltpu.make_async_copy(feat_hbm, feat_v, in_sem.at[0])
    cot_in = pltpu.make_async_copy(cot_hbm, cot_v, in_sem.at[1])
    w_in = pltpu.make_async_copy(w_hbm, w_ref, in_sem.at[2])
    occ_in = pltpu.make_async_copy(occ_hbm, occ_ref, in_sem.at[3])
    nb_in = pltpu.make_async_copy(nb_hbm, nb_ref, in_sem.at[4])
    occ_in.start()
    feat_in.start()
    cot_in.start()
    w_in.start()
    nb_in.start()

    barrier = pltpu.get_barrier_semaphore()
    signals = 0
    for dev in [up_dev, down_dev, pair_dev]:
        pl.semaphore_signal(barrier, inc=1, device_id=dev, device_id_type=MESH)
        signals += 1
    for j in range(1, N_XY):
        pl.semaphore_signal(barrier, inc=1, device_id=xy_peer(j)[1], device_id_type=MESH)
        signals += 1
    for j in range(1, N_Z):
        pl.semaphore_signal(barrier, inc=1, device_id=z_peer(j), device_id_type=MESH)
        signals += 1

    def occ_at(z):
        return occ_ref[:, pl.ds(z * PLANE, PLANE)].astype(F32)

    occ_in.wait()
    feat_in.wait()
    for n, z in enumerate((BS - 1, 0)):
        halo_send[0, n] = (feat_v[:, z * PLANE : (z + 1) * PLANE].astype(F32) * occ_at(z)).astype(BF)
    pl.semaphore_wait(barrier, signals)

    def halo_copy(field, n):
        return pltpu.make_async_remote_copy(
            src_ref=halo_send.at[field, n],
            dst_ref=halo_recv.at[field, n],
            send_sem=halo_ssem.at[field, n],
            recv_sem=halo_rsem.at[field, n],
            device_id=(up_dev, down_dev)[n],
            device_id_type=MESH,
        )

    halos = [[halo_copy(field, n) for n in range(2)] for field in range(2)]
    halos[0][0].start()
    halos[0][1].start()

    def fill(s9, plane, layer, slot):
        lanes = pl.ds(pl.multiple_of(slot * PLANE, PLANE), PLANE)
        for k, moved in enumerate(spread(plane, x_iota)):
            s9[k * C : (k + 1) * C, lanes] = moved.astype(BF) * mask_v[layer, k]

    cot_in.wait()
    for n, z in enumerate((BS - 1, 0)):
        halo_send[1, n] = (cot_v[:, z * PLANE : (z + 1) * PLANE].astype(F32) * occ_at(z)).astype(BF)
    halos[1][0].start()
    halos[1][1].start()

    nb_in.wait()
    lane = lax.broadcasted_iota(jnp.int32, (C, PLANE), 1)
    x_iota = lane % BS
    y_iota = lane // BS
    for layer in range(3):
        flag = [jnp.where(nb_ref[0, 9 * layer + k] >= 0, 1.0, 0.0).astype(F32) for k in range(9)]
        for dy in (-1, 0, 1):
            y_out = y_iota == (BS - 1 if dy == 1 else 0 if dy == -1 else -1)
            for dx in (-1, 0, 1):
                x_out = x_iota == (BS - 1 if dx == 1 else 0 if dx == -1 else -1)

                def at(a, b):
                    return flag[3 * (a + 1) + b + 1]

                inner = jnp.where(x_out, at(0, dx), at(0, 0))
                outer = jnp.where(x_out, at(dy, dx), at(dy, 0))
                mask_v[layer, 3 * (dy + 1) + dx + 1] = jnp.where(y_out, outer, inner).astype(BF)


    def own_planes(z, carry):
        z0 = pl.multiple_of(z * PLANE, PLANE)
        occ = occ_ref[:, pl.ds(z0, PLANE)].astype(F32)
        live = feat_v[:, pl.ds(z0, PLANE)].astype(F32) * occ
        fill(s9f, live, 1, z + 1)
        ups = (cot_v[:, pl.ds(z0, PLANE)].astype(F32) * occ).astype(BF)
        for dz in range(3):
            u3[dz * C : (dz + 1) * C, pl.ds(pl.multiple_of((z + dz) * PLANE, PLANE), PLANE)] = ups
        return carry

    part[24:30, :, C:128] = jnp.zeros((6, 32, C), F32)
    part[30:32] = jnp.zeros((2, 32, 128), F32)
    u3[0:C, V : V + PLANE] = jnp.zeros((C, PLANE), BF)
    u3[2 * C : 3 * C, PLANE : 2 * PLANE] = jnp.zeros((C, PLANE), BF)
    lax.fori_loop(0, BS, own_planes, 0)

    def columns(t):
        return t * PLANE, min(PLANE, TAPS * C - t * PLANE)

    def chunk(t, n, r):
        return (2 * t + n // 128) * 6 + r

    nt = (((1,), (1,)), ((), ()))
    for t in range(3):
        base, width = columns(t)
        g = lax.dot_general(
            u3[:, PLANE : PLANE + V], s9f[base : base + width, PLANE : PLANE + V], nt,
            preferred_element_type=F32,
        )
        for n in range(0, width, 128):
            w = min(128, width - n)
            for r in range(6):
                part[chunk(t, n, r), :, 0:w] = g[32 * r : 32 * r + 32, n : n + w]

    for n, layer in ((0, 0), (1, 2)):
        halos[0][n].wait_recv()
        slot = layer * (BS + 1) // 2
        fill(s9f, halo_recv[0, n].astype(F32), layer, slot)
        edge = u3[layer * C : layer * C + C, slot * PLANE : slot * PLANE + PLANE]
        for t in range(3):
            base, width = columns(t)
            g = lax.dot_general(
                edge, s9f[base : base + width, slot * PLANE : slot * PLANE + PLANE], nt,
                preferred_element_type=F32,
            )
            for m in range(0, width, 128):
                w = min(128, width - m)
                for h in range(2):
                    part[chunk(t, m, 2 * layer + h), :, 0:w] += g[32 * h : 32 * h + 32, m : m + w]

    pair = pltpu.make_async_remote_copy(
        src_ref=part.at[pl.ds((1 - cc) * N_XY, N_XY)],
        dst_ref=pair_recv,
        send_sem=ar_ssem.at[0],
        recv_sem=ar_rsem.at[0],
        device_id=pair_dev,
        device_id_type=MESH,
    )
    pair.start()

    pair.wait_recv()
    half[...] = part[pl.ds(cc * N_XY, N_XY)] + pair_recv[...]

    def xy_copy(j):
        i, dev = xy_peer(j)
        return pltpu.make_async_remote_copy(
            src_ref=half.at[i],
            dst_ref=xy_recv.at[j],
            send_sem=ar_ssem.at[j],
            recv_sem=ar_rsem.at[j],
            device_id=dev,
            device_id_type=MESH,
        )

    xy_order = [10, 9, 11, 6, 7, 5, 14, 8, 2, 13, 3, 1, 15, 4, 12]
    xy_copies = {j: xy_copy(j) for j in xy_order}
    for j in xy_order:
        xy_copies[j].start()

    w_in.wait()
    for k in range(27):
        dz, j = k // 9, k % 9
        wf[dz * C : (dz + 1) * C, j * C : (j + 1) * C] = w_ref[k]
        wb[dz * C : (dz + 1) * C, j * C : (j + 1) * C] = jnp.transpose(w_ref[26 - k].astype(F32)).astype(BF)

    def convolve(weights, s9, dst):
        step = 6 * PLANE
        for n in range(0, EXT, step):
            products[:, n : n + step] = jnp.dot(
                weights[...], s9[:, n : n + step], preferred_element_type=F32
            )

        def combine(z, carry):
            z0 = pl.multiple_of(z * PLANE, PLANE)
            acc = products[0:C, pl.ds(z0, PLANE)]
            for dz in (1, 2):
                acc += products[dz * C : dz * C + C, pl.ds(pl.multiple_of(z0 + dz * PLANE, PLANE), PLANE)]
            dst[:, pl.ds(z0, PLANE)] = (acc * occ_ref[:, pl.ds(z0, PLANE)].astype(F32)).astype(BF)
            return carry

        lax.fori_loop(0, BS, combine, 0)

    convolve(wf, s9f, out_v)
    out_copy = pltpu.make_async_copy(out_v, out_hbm, out_sem.at[0])
    out_copy.start()

    for j in xy_order:
        xy_copies[j].wait_recv()
    own[...] = half[xy]
    for j in range(1, N_XY):
        own[...] += xy_recv[j]

    def z_copy(j):
        return pltpu.make_async_remote_copy(
            src_ref=own,
            dst_ref=z_recv.at[j],
            send_sem=ar_ssem.at[16 + j],
            recv_sem=ar_rsem.at[16 + j],
            device_id=z_peer(j),
            device_id_type=MESH,
        )

    z_order = [4, 3, 5, 2, 6, 1, 7]
    z_copies = {j: z_copy(j) for j in z_order}
    for j in z_order:
        z_copies[j].start()

    halos[1][0].wait_recv()
    halos[1][1].wait_recv()
    fill(s9u, halo_recv[1, 0].astype(F32), 0, 0)
    fill(s9u, halo_recv[1, 1].astype(F32), 2, BS + 1)

    def up_planes(z, carry):
        z0 = pl.multiple_of((z + 1) * PLANE, PLANE)
        fill(s9u, u3[C : 2 * C, pl.ds(z0, PLANE)].astype(F32), 1, z + 1)
        return carry

    lax.fori_loop(0, BS, up_planes, 0)
    convolve(wb, s9u, gin_v)
    gin_copy = pltpu.make_async_copy(gin_v, gin_hbm, out_sem.at[1])
    gin_copy.start()

    for j in z_order:
        z_copies[j].wait_recv()
    z_recv[0] = own[...]
    total[...] = z_recv[cz]
    for s in range(1, N_Z):
        total[...] += z_recv[lax.rem(cz + N_Z - s, N_Z)]

    def back_copy(j):
        i, dev = xy_peer(j)
        return pltpu.make_async_remote_copy(
            src_ref=total,
            dst_ref=final.at[cc * N_XY + xy],
            send_sem=ar_ssem.at[24 + j],
            recv_sem=ar_rsem.at[24 + j],
            device_id=dev,
            device_id_type=MESH,
        )

    back_copies = {j: back_copy(j) for j in xy_order}
    for j in xy_order:
        back_copies[j].start()
    final[cc * N_XY + xy] = total[...]

    def forward(i):
        slot = final.at[cc * N_XY + i]
        copy = pltpu.make_async_remote_copy(
            src_ref=slot, dst_ref=slot, send_sem=ar_ssem.at[40 + i], recv_sem=ar_rsem.at[40 + i],
            device_id=pair_dev, device_id_type=MESH,
        )
        copy.start()
        return copy

    forwards = [forward(xy)]
    for j in reversed(xy_order):
        back_copies[j].wait_recv()
        forwards.append(forward(lax.rem(xy + N_XY - j, N_XY)))
    for copy in forwards:
        copy.wait_recv()
    gw_copy = pltpu.make_async_copy(final, gw_hbm, out_sem.at[2])
    gw_copy.start()

    pair.wait_send()
    for copy in forwards:
        copy.wait_send()
    for j in xy_order:
        xy_copies[j].wait_send()
        back_copies[j].wait_send()
    for j in z_order:
        z_copies[j].wait_send()
    for field in range(2):
        for n in range(2):
            halos[field][n].wait_send()
    out_copy.wait()
    gin_copy.wait()
    gw_copy.wait()


def deliver(out_ref, gin_ref, final_ref, out_hbm, gin_hbm, gw_hbm, final_v, gw_v, sems):
    copies = [
        pltpu.make_async_copy(final_ref, final_v, sems.at[0]),
        pltpu.make_async_copy(out_ref, out_hbm, sems.at[1]),
        pltpu.make_async_copy(gin_ref, gin_hbm, sems.at[2]),
    ]
    for copy in copies:
        copy.start()
    copies[0].wait()
    for k in range(27):
        dz, j = k // 9, k % 9
        for h in range(2):
            gw_v[k, 32 * h : 32 * h + 32, :] = final_v[(j // 2) * 6 + 2 * dz + h, :, (j % 2) * C : (j % 2 + 1) * C]
    gw_copy = pltpu.make_async_copy(gw_v, gw_hbm, sems.at[3])
    gw_copy.start()
    copies[1].wait()
    copies[2].wait()
    gw_copy.wait()


def local(features, cotangent, weight, neighbours, occupancy):
    hbm = pl.BlockSpec(memory_space=pltpu.HBM)
    anywhere = pl.BlockSpec(memory_space=pl.ANY)
    field = jax.ShapeDtypeStruct((C, V), BF)
    output, grad_input, chunks = pl.pallas_call(
        kernel,
        out_shape=(field, field, jax.ShapeDtypeStruct((32, 32, 128), F32)),
        in_specs=[hbm, hbm, hbm, hbm, hbm],
        out_specs=(anywhere, anywhere, anywhere),
        scratch_shapes=[
            pltpu.VMEM((C, V), BF),
            pltpu.VMEM((C, V), BF),
            pltpu.VMEM((27, C, C), BF),
            pltpu.SMEM((1, 27), jnp.int32),
            pltpu.VMEM((1, V), jnp.int32),
            pltpu.VMEM((C, V), BF),
            pltpu.VMEM((C, V), BF),
            pltpu.VMEM((3 * C, EXT), F32),
            pltpu.VMEM((3, TAPS, C, PLANE), BF),
            pltpu.VMEM((TAPS * C, EXT), BF),
            pltpu.VMEM((TAPS * C, EXT), BF),
            pltpu.VMEM((3 * C, EXT), BF),
            pltpu.VMEM((3 * C, TAPS * C), BF),
            pltpu.VMEM((3 * C, TAPS * C), BF),
            pltpu.VMEM((2, 2, C, PLANE), BF),
            pltpu.VMEM((2, 2, C, PLANE), BF),
            pltpu.VMEM((32, 32, 128), F32),
            pltpu.VMEM((16, 32, 128), F32),
            pltpu.VMEM((16, 32, 128), F32),
            pltpu.VMEM((16, 32, 128), F32),
            pltpu.VMEM((32, 128), F32),
            pltpu.VMEM((8, 32, 128), F32),
            pltpu.VMEM((32, 128), F32),
            pltpu.VMEM((32, 32, 128), F32),
            pltpu.SemaphoreType.DMA((5,)),
            pltpu.SemaphoreType.DMA((3,)),
            pltpu.SemaphoreType.DMA((2, 2)),
            pltpu.SemaphoreType.DMA((2, 2)),
            pltpu.SemaphoreType.DMA((56,)),
            pltpu.SemaphoreType.DMA((56,)),
        ],
        compiler_params=pltpu.CompilerParams(
            collective_id=0, has_side_effects=True, vmem_limit_bytes=40 * 2**20
        ),
    )(
        pltpu.with_memory_space_constraint(features.reshape(C, V), pltpu.HBM),
        pltpu.with_memory_space_constraint(cotangent.reshape(C, V), pltpu.HBM),
        pltpu.with_memory_space_constraint(weight, pltpu.HBM),
        pltpu.with_memory_space_constraint(neighbours.reshape(1, 27), pltpu.HBM),
        pltpu.with_memory_space_constraint(occupancy.reshape(1, V), pltpu.HBM),
    )
    output, grad_input, grad_weight = pl.pallas_call(
        deliver,
        out_shape=(field, field, jax.ShapeDtypeStruct((27, C, C), F32)),
        in_specs=[anywhere, anywhere, anywhere],
        out_specs=(hbm, hbm, hbm),
        scratch_shapes=[
            pltpu.VMEM((32, 32, 128), F32),
            pltpu.VMEM((27, C, C), F32),
            pltpu.SemaphoreType.DMA((4,)),
        ],
        compiler_params=pltpu.CompilerParams(vmem_limit_bytes=16 * 2**20),
    )(output, grad_input, chunks)
    return output.reshape(1, 1, C, V), grad_input.reshape(1, 1, C, V), grad_weight


def solution(mesh):
    in_specs = (
        P("scan", "brick", None, None),
        P("scan", "brick", None, None),
        P(),
        P("scan", "brick", None),
        P("scan", "brick", None),
    )
    out_specs = (P("scan", "brick", None, None), P("scan", "brick", None, None), P())
    return jax.shard_map(local, mesh=mesh, in_specs=in_specs, out_specs=out_specs, check_vma=False)
```

```python
import jax
import jax.numpy as jnp
from jax import lax
from jax.experimental import pallas as pl
from jax.experimental.pallas import tpu as pltpu
from jax.sharding import PartitionSpec as P

C = 64
BS = 16
PLANE = BS * BS
V = BS * PLANE
EXT = (BS + 2) * PLANE
TAPS = 9
BF = jnp.bfloat16
F32 = jnp.float32
MESH = pl.DeviceIdType.MESH
N_CORE, N_X, N_Y, N_Z = 2, 4, 4, 8
N_BRICK = N_Y * N_Z
N_XY = N_X * N_Y


def spread(plane, x_iota):
    left = jnp.where(x_iota == 0, pltpu.roll(plane, PLANE - 15, 1), pltpu.roll(plane, 1, 1))
    right = jnp.where(x_iota == BS - 1, pltpu.roll(plane, 15, 1), pltpu.roll(plane, PLANE - 1, 1))
    shifted = []
    for dy in (-1, 0, 1):
        for base in (left, plane, right):
            shifted.append(base if dy == 0 else pltpu.roll(base, (-dy * BS) % PLANE, 1))
    return shifted


def kernel(
    feat_hbm, cot_hbm, w_hbm, nb_hbm, occ_hbm,
    out_hbm, gin_hbm, chunk_ref,
    feat_v, cot_v, edge_v, w_ref, nb_ref, occ_ref, out_v, gin_v, products, mask_v, s9f, s9u, u3, wf, wb,
    halo_send, halo_recv, part, pair_recv, half, xy_recv, own, z_recv, total, final,
    in_sem, out_sem, halo_ssem, halo_rsem, ar_ssem, ar_rsem, round_sem,
):
    scan = lax.axis_index("scan")
    brick = lax.axis_index("brick")
    cx, cc = scan // N_CORE, scan % N_CORE
    cz, cy = brick // N_Y, brick % N_Y
    xy = cx * N_Y + cy
    up_dev = (scan, lax.rem(brick + 1, N_BRICK))
    down_dev = (scan, lax.rem(brick + N_BRICK - 1, N_BRICK))
    pair_dev = (cx * N_CORE + 1 - cc, brick)

    def xy_peer(j):
        i = lax.rem(xy + j, N_XY)
        return i, ((i // N_Y) * N_CORE + cc, cz * N_Y + lax.rem(i, N_Y))

    def z_peer(j):
        return (scan, lax.rem(cz + j, N_Z) * N_Y + cy)

    def edge_in(hbm, n):
        lanes = pl.ds((BS - 1) * PLANE * (1 - n), PLANE)
        return pltpu.make_async_copy(hbm.at[:, lanes], edge_v.at[n], in_sem.at[5 + n])

    edges = [edge_in(feat_hbm, n) for n in range(2)]
    feat_in = pltpu.make_async_copy(feat_hbm, feat_v, in_sem.at[0])
    cot_in = pltpu.make_async_copy(cot_hbm, cot_v, in_sem.at[1])
    w_in = pltpu.make_async_copy(w_hbm, w_ref, in_sem.at[2])
    occ_in = pltpu.make_async_copy(occ_hbm, occ_ref, in_sem.at[3])
    nb_in = pltpu.make_async_copy(nb_hbm, nb_ref, in_sem.at[4])
    occ_in.start()
    edges[0].start()
    edges[1].start()
    feat_in.start()
    cot_in.start()
    w_in.start()
    nb_in.start()

    def around(dx, dy, dz):
        return (
            lax.rem(cx + dx, N_X) * N_CORE + cc,
            lax.rem(cz + dz, N_Z) * N_Y + lax.rem(cy + dy, N_Y),
        )

    x_line = [around(dx, 0, 0) for dx in (2, 1, 3)]
    y_line = [around(0, dy, 0) for dy in (2, 1, 3)]
    z_near = [around(0, 0, 1), around(0, 0, N_Z - 1)]
    z_next = [around(0, 0, 2), around(0, 0, N_Z - 2)]

    barrier = pltpu.get_barrier_semaphore()
    near = x_line + y_line + z_near + [up_dev, down_dev, pair_dev]
    for dev in near:
        pl.semaphore_signal(barrier, inc=1, device_id=dev, device_id_type=MESH)

    def occ_at(z):
        return occ_ref[:, pl.ds(z * PLANE, PLANE)].astype(F32)

    occ_in.wait()
    for n, z in enumerate((BS - 1, 0)):
        edges[n].wait()
        halo_send[0, n] = (edge_v[n].astype(F32) * occ_at(z)).astype(BF)
    pl.semaphore_wait(barrier, len(near))

    def halo_copy(field, n):
        return pltpu.make_async_remote_copy(
            src_ref=halo_send.at[field, n],
            dst_ref=halo_recv.at[field, n],
            send_sem=halo_ssem.at[field, n],
            recv_sem=halo_rsem.at[field, n],
            device_id=(up_dev, down_dev)[n],
            device_id_type=MESH,
        )

    halos = [[halo_copy(field, n) for n in range(2)] for field in range(2)]
    halos[0][0].start()
    halos[0][1].start()
    for dev in x_line + z_near:
        pl.semaphore_signal(round_sem.at[0], inc=1, device_id=dev, device_id_type=MESH)

    def fill(s9, plane, layer, slot):
        lanes = pl.ds(pl.multiple_of(slot * PLANE, PLANE), PLANE)
        for k, moved in enumerate(spread(plane, x_iota)):
            s9[k * C : (k + 1) * C, lanes] = moved.astype(BF) * mask_v[layer, k]

    feat_in.wait()
    cot_in.wait()
    for n, z in enumerate((BS - 1, 0)):
        halo_send[1, n] = (cot_v[:, z * PLANE : (z + 1) * PLANE].astype(F32) * occ_at(z)).astype(BF)
    halos[1][0].start()
    halos[1][1].start()

    nb_in.wait()
    lane = lax.broadcasted_iota(jnp.int32, (C, PLANE), 1)
    x_iota = lane % BS
    y_iota = lane // BS
    for layer in range(3):
        flag = [jnp.where(nb_ref[0, 9 * layer + k] >= 0, 1.0, 0.0).astype(F32) for k in range(9)]
        for dy in (-1, 0, 1):
            y_out = y_iota == (BS - 1 if dy == 1 else 0 if dy == -1 else -1)
            for dx in (-1, 0, 1):
                x_out = x_iota == (BS - 1 if dx == 1 else 0 if dx == -1 else -1)

                def at(a, b):
                    return flag[3 * (a + 1) + b + 1]

                inner = jnp.where(x_out, at(0, dx), at(0, 0))
                outer = jnp.where(x_out, at(dy, dx), at(dy, 0))
                mask_v[layer, 3 * (dy + 1) + dx + 1] = jnp.where(y_out, outer, inner).astype(BF)


    def own_planes(z, carry):
        z0 = pl.multiple_of(z * PLANE, PLANE)
        occ = occ_ref[:, pl.ds(z0, PLANE)].astype(F32)
        live = feat_v[:, pl.ds(z0, PLANE)].astype(F32) * occ
        fill(s9f, live, 1, z + 1)
        ups = (cot_v[:, pl.ds(z0, PLANE)].astype(F32) * occ).astype(BF)
        for dz in range(3):
            u3[dz * C : (dz + 1) * C, pl.ds(pl.multiple_of((z + dz) * PLANE, PLANE), PLANE)] = ups
        return carry

    part[24:30, :, C:128] = jnp.zeros((6, 32, C), F32)
    part[30:32] = jnp.zeros((2, 32, 128), F32)
    u3[0:C, V : V + PLANE] = jnp.zeros((C, PLANE), BF)
    u3[2 * C : 3 * C, PLANE : 2 * PLANE] = jnp.zeros((C, PLANE), BF)
    lax.fori_loop(0, BS, own_planes, 0)

    def columns(t):
        return t * PLANE, min(PLANE, TAPS * C - t * PLANE)

    def chunk(t, n, r):
        return (2 * t + n // 128) * 6 + r

    nt = (((1,), (1,)), ((), ()))
    for t in range(3):
        base, width = columns(t)
        g = lax.dot_general(
            u3[:, PLANE : PLANE + V], s9f[base : base + width, PLANE : PLANE + V], nt,
            preferred_element_type=F32,
        )
        for n in range(0, width, 128):
            w = min(128, width - n)
            for r in range(6):
                part[chunk(t, n, r), :, 0:w] = g[32 * r : 32 * r + 32, n : n + w]

    pl.semaphore_wait(round_sem.at[0], len(x_line) + len(z_near))
    for dev in z_next:
        pl.semaphore_signal(round_sem.at[1], inc=1, device_id=dev, device_id_type=MESH)

    for n, layer in ((0, 0), (1, 2)):
        halos[0][n].wait_recv()
        slot = layer * (BS + 1) // 2
        fill(s9f, halo_recv[0, n].astype(F32), layer, slot)
        edge = u3[layer * C : layer * C + C, slot * PLANE : slot * PLANE + PLANE]
        for t in range(3):
            base, width = columns(t)
            g = lax.dot_general(
                edge, s9f[base : base + width, slot * PLANE : slot * PLANE + PLANE], nt,
                preferred_element_type=F32,
            )
            for m in range(0, width, 128):
                w = min(128, width - m)
                for h in range(2):
                    part[chunk(t, m, 2 * layer + h), :, 0:w] += g[32 * h : 32 * h + 32, m : m + w]

    pair = pltpu.make_async_remote_copy(
        src_ref=part.at[pl.ds((1 - cc) * N_XY, N_XY)],
        dst_ref=pair_recv,
        send_sem=ar_ssem.at[0],
        recv_sem=ar_rsem.at[0],
        device_id=pair_dev,
        device_id_type=MESH,
    )
    pair.start()

    pair.wait_recv()
    half[...] = part[pl.ds(cc * N_XY, N_XY)] + pair_recv[...]

    def xy_copy(j):
        i, dev = xy_peer(j)
        return pltpu.make_async_remote_copy(
            src_ref=half.at[i],
            dst_ref=xy_recv.at[j],
            send_sem=ar_ssem.at[j],
            recv_sem=ar_rsem.at[j],
            device_id=dev,
            device_id_type=MESH,
        )

    xy_order = [10, 9, 11, 6, 7, 5, 14, 8, 2, 13, 3, 1, 15, 4, 12]
    xy_copies = {j: xy_copy(j) for j in xy_order}
    for j in xy_order:
        xy_copies[j].start()

    w_in.wait()
    for k in range(27):
        dz, j = k // 9, k % 9
        wf[dz * C : (dz + 1) * C, j * C : (j + 1) * C] = w_ref[k]
        wb[dz * C : (dz + 1) * C, j * C : (j + 1) * C] = jnp.transpose(w_ref[26 - k].astype(F32)).astype(BF)

    def convolve(weights, s9, dst):
        step = 6 * PLANE
        for n in range(0, EXT, step):
            products[:, n : n + step] = jnp.dot(
                weights[...], s9[:, n : n + step], preferred_element_type=F32
            )

        def combine(z, carry):
            z0 = pl.multiple_of(z * PLANE, PLANE)
            acc = products[0:C, pl.ds(z0, PLANE)]
            for dz in (1, 2):
                acc += products[dz * C : dz * C + C, pl.ds(pl.multiple_of(z0 + dz * PLANE, PLANE), PLANE)]
            dst[:, pl.ds(z0, PLANE)] = (acc * occ_ref[:, pl.ds(z0, PLANE)].astype(F32)).astype(BF)
            return carry

        lax.fori_loop(0, BS, combine, 0)

    convolve(wf, s9f, out_v)
    out_copy = pltpu.make_async_copy(out_v, out_hbm, out_sem.at[0])
    out_copy.start()

    for j in xy_order:
        xy_copies[j].wait_recv()
    own[...] = half[xy]
    for j in range(1, N_XY):
        own[...] += xy_recv[j]

    def z_copy(j):
        return pltpu.make_async_remote_copy(
            src_ref=own,
            dst_ref=z_recv.at[j],
            send_sem=ar_ssem.at[16 + j],
            recv_sem=ar_rsem.at[16 + j],
            device_id=z_peer(j),
            device_id_type=MESH,
        )

    pl.semaphore_wait(round_sem.at[1], len(z_next))
    z_order = [4, 3, 5, 2, 6, 1, 7]
    z_copies = {j: z_copy(j) for j in z_order}
    for j in z_order:
        z_copies[j].start()

    halos[1][0].wait_recv()
    halos[1][1].wait_recv()
    fill(s9u, halo_recv[1, 0].astype(F32), 0, 0)
    fill(s9u, halo_recv[1, 1].astype(F32), 2, BS + 1)

    def up_planes(z, carry):
        z0 = pl.multiple_of((z + 1) * PLANE, PLANE)
        fill(s9u, u3[C : 2 * C, pl.ds(z0, PLANE)].astype(F32), 1, z + 1)
        return carry

    lax.fori_loop(0, BS, up_planes, 0)
    convolve(wb, s9u, gin_v)
    gin_copy = pltpu.make_async_copy(gin_v, gin_hbm, out_sem.at[1])
    gin_copy.start()

    for j in z_order:
        z_copies[j].wait_recv()
    z_recv[0] = own[...]
    total[...] = z_recv[cz]
    for s in range(1, N_Z):
        total[...] += z_recv[lax.rem(cz + N_Z - s, N_Z)]

    def back_copy(j):
        i, dev = xy_peer(j)
        return pltpu.make_async_remote_copy(
            src_ref=total,
            dst_ref=final.at[cc * N_XY + xy],
            send_sem=ar_ssem.at[24 + j],
            recv_sem=ar_rsem.at[24 + j],
            device_id=dev,
            device_id_type=MESH,
        )

    back_copies = {j: back_copy(j) for j in xy_order}
    for j in xy_order:
        back_copies[j].start()
    final[cc * N_XY + xy] = total[...]

    def forward(i):
        slot = final.at[cc * N_XY + i]
        copy = pltpu.make_async_remote_copy(
            src_ref=slot, dst_ref=slot, send_sem=ar_ssem.at[40 + i], recv_sem=ar_rsem.at[40 + i],
            device_id=pair_dev, device_id_type=MESH,
        )
        copy.start()
        return copy

    forwards = {0: forward(xy)}
    chunk_ref[cc * N_XY + xy] = total[...]
    for j in reversed(xy_order):
        back_copies[j].wait_recv()
        i = lax.rem(xy + N_XY - j, N_XY)
        forwards[j] = forward(i)
        chunk_ref[cc * N_XY + i] = final[cc * N_XY + i]
    for j, copy in forwards.items():
        copy.wait_recv()
    other = pl.ds((1 - cc) * N_XY, N_XY)
    chunk_ref[other] = final[other]

    pair.wait_send()
    for copy in forwards.values():
        copy.wait_send()
    for j in xy_order:
        xy_copies[j].wait_send()
        back_copies[j].wait_send()
    for j in z_order:
        z_copies[j].wait_send()
    for field in range(2):
        for n in range(2):
            halos[field][n].wait_send()
    out_copy.wait()
    gin_copy.wait()


def deliver(out_ref, gin_ref, chunk_ref, out_hbm, gin_hbm, gw_hbm, gw_v, sems):
    copies = [
        pltpu.make_async_copy(out_ref, out_hbm, sems.at[0]),
        pltpu.make_async_copy(gin_ref, gin_hbm, sems.at[1]),
    ]
    for copy in copies:
        copy.start()
    for k in range(27):
        dz, j = k // 9, k % 9
        for h in range(2):
            gw_v[k, 32 * h : 32 * h + 32, :] = chunk_ref[(j // 2) * 6 + 2 * dz + h, :, (j % 2) * C : (j % 2 + 1) * C]
    gw_copy = pltpu.make_async_copy(gw_v, gw_hbm, sems.at[2])
    gw_copy.start()
    for copy in copies:
        copy.wait()
    gw_copy.wait()


def local(features, cotangent, weight, neighbours, occupancy):
    hbm = pl.BlockSpec(memory_space=pltpu.HBM)
    vmem = pl.BlockSpec(memory_space=pltpu.VMEM)
    anywhere = pl.BlockSpec(memory_space=pl.ANY)
    field = jax.ShapeDtypeStruct((C, V), BF)
    output, grad_input, chunks = pl.pallas_call(
        kernel,
        out_shape=(field, field, jax.ShapeDtypeStruct((32, 32, 128), F32)),
        in_specs=[hbm, hbm, hbm, hbm, hbm],
        out_specs=(anywhere, anywhere, vmem),
        scratch_shapes=[
            pltpu.VMEM((C, V), BF),
            pltpu.VMEM((C, V), BF),
            pltpu.VMEM((2, C, PLANE), BF),
            pltpu.VMEM((27, C, C), BF),
            pltpu.SMEM((1, 27), jnp.int32),
            pltpu.VMEM((1, V), jnp.int32),
            pltpu.VMEM((C, V), BF),
            pltpu.VMEM((C, V), BF),
            pltpu.VMEM((3 * C, EXT), F32),
            pltpu.VMEM((3, TAPS, C, PLANE), BF),
            pltpu.VMEM((TAPS * C, EXT), BF),
            pltpu.VMEM((TAPS * C, EXT), BF),
            pltpu.VMEM((3 * C, EXT), BF),
            pltpu.VMEM((3 * C, TAPS * C), BF),
            pltpu.VMEM((3 * C, TAPS * C), BF),
            pltpu.VMEM((2, 2, C, PLANE), BF),
            pltpu.VMEM((2, 2, C, PLANE), BF),
            pltpu.VMEM((32, 32, 128), F32),
            pltpu.VMEM((16, 32, 128), F32),
            pltpu.VMEM((16, 32, 128), F32),
            pltpu.VMEM((16, 32, 128), F32),
            pltpu.VMEM((32, 128), F32),
            pltpu.VMEM((8, 32, 128), F32),
            pltpu.VMEM((32, 128), F32),
            pltpu.VMEM((32, 32, 128), F32),
            pltpu.SemaphoreType.DMA((7,)),
            pltpu.SemaphoreType.DMA((3,)),
            pltpu.SemaphoreType.DMA((2, 2)),
            pltpu.SemaphoreType.DMA((2, 2)),
            pltpu.SemaphoreType.DMA((56,)),
            pltpu.SemaphoreType.DMA((56,)),
            pltpu.SemaphoreType.REGULAR((2,)),
        ],
        compiler_params=pltpu.CompilerParams(
            collective_id=0, has_side_effects=True, vmem_limit_bytes=40 * 2**20
        ),
    )(
        pltpu.with_memory_space_constraint(features.reshape(C, V), pltpu.HBM),
        pltpu.with_memory_space_constraint(cotangent.reshape(C, V), pltpu.HBM),
        pltpu.with_memory_space_constraint(weight, pltpu.HBM),
        pltpu.with_memory_space_constraint(neighbours.reshape(1, 27), pltpu.HBM),
        pltpu.with_memory_space_constraint(occupancy.reshape(1, V), pltpu.HBM),
    )
    output, grad_input, grad_weight = pl.pallas_call(
        deliver,
        out_shape=(field, field, jax.ShapeDtypeStruct((27, C, C), F32)),
        in_specs=[anywhere, anywhere, vmem],
        out_specs=(hbm, hbm, hbm),
        scratch_shapes=[
            pltpu.VMEM((27, C, C), F32),
            pltpu.SemaphoreType.DMA((3,)),
        ],
        compiler_params=pltpu.CompilerParams(vmem_limit_bytes=16 * 2**20),
    )(output, grad_input, chunks)
    return output.reshape(1, 1, C, V), grad_input.reshape(1, 1, C, V), grad_weight


def solution(mesh):
    in_specs = (
        P("scan", "brick", None, None),
        P("scan", "brick", None, None),
        P(),
        P("scan", "brick", None),
        P("scan", "brick", None),
    )
    out_specs = (P("scan", "brick", None, None), P("scan", "brick", None, None), P())
    return jax.shard_map(local, mesh=mesh, in_specs=in_specs, out_specs=out_specs, check_vma=False)
```

```python
import jax
import jax.numpy as jnp
from jax import lax
from jax.experimental import pallas as pl
from jax.experimental.pallas import tpu as pltpu
from jax.sharding import PartitionSpec as P

C = 64
BS = 16
PLANE = BS * BS
V = BS * PLANE
EXT = (BS + 2) * PLANE
TAPS = 9
BF = jnp.bfloat16
F32 = jnp.float32
MESH = pl.DeviceIdType.MESH
N_CORE, N_X, N_Y, N_Z = 2, 4, 4, 8
N_BRICK = N_Y * N_Z
N_XY = N_X * N_Y
UNROLL = 4
SUBS = 1
SUB = 32 // SUBS
UP_SPLIT = 16
EARLY = 4


def spread(plane, x_iota):
    left = jnp.where(x_iota == 0, pltpu.roll(plane, PLANE - 15, 1), pltpu.roll(plane, 1, 1))
    right = jnp.where(x_iota == BS - 1, pltpu.roll(plane, 15, 1), pltpu.roll(plane, PLANE - 1, 1))
    shifted = []
    for dy in (-1, 0, 1):
        for base in (left, plane, right):
            shifted.append(base if dy == 0 else pltpu.roll(base, (-dy * BS) % PLANE, 1))
    return shifted


def kernel(
    feat_hbm, cot_hbm, w_hbm, nb_hbm, occ_hbm,
    out_hbm, gin_hbm, chunk_ref,
    feat_v, cot_v, edge_v, w_ref, nb_ref, occ_ref, out_v, gin_v, products, mask_v, s9f, s9u, u3, wf, wb,
    halo_send, halo_recv, part, pair_recv, half, xy_recv, own, z_recv, total, final,
    in_sem, out_sem, halo_ssem, halo_rsem, pair_ssem, pair_rsem, xy_ssem, xy_rsem, z_ssem, z_rsem, back_ssem, back_rsem, on_ssem, on_rsem, round_sem,
):
    scan = lax.axis_index("scan")
    brick = lax.axis_index("brick")
    cx, cc = scan // N_CORE, scan % N_CORE
    cz, cy = brick // N_Y, brick % N_Y
    xy = cx * N_Y + cy
    up_dev = (scan, lax.rem(brick + 1, N_BRICK))
    down_dev = (scan, lax.rem(brick + N_BRICK - 1, N_BRICK))
    pair_dev = (cx * N_CORE + 1 - cc, brick)

    def xy_peer(j):
        i = lax.rem(xy + j, N_XY)
        return i, ((i // N_Y) * N_CORE + cc, cz * N_Y + lax.rem(i, N_Y))

    def z_peer(j):
        return (scan, lax.rem(cz + j, N_Z) * N_Y + cy)

    def edge_in(hbm, n):
        lanes = pl.ds((BS - 1) * PLANE * (1 - n), PLANE)
        return pltpu.make_async_copy(hbm.at[:, lanes], edge_v.at[n], in_sem.at[5 + n])

    edges = [edge_in(feat_hbm, n) for n in range(2)]
    feat_in = pltpu.make_async_copy(feat_hbm, feat_v, in_sem.at[0])
    cot_in = pltpu.make_async_copy(cot_hbm, cot_v, in_sem.at[1])
    w_in = pltpu.make_async_copy(w_hbm, w_ref, in_sem.at[2])
    occ_in = pltpu.make_async_copy(occ_hbm, occ_ref, in_sem.at[3])
    nb_in = pltpu.make_async_copy(nb_hbm, nb_ref, in_sem.at[4])
    occ_in.start()
    edges[0].start()
    edges[1].start()

    cot_in.start()
    w_in.start()
    nb_in.start()

    def around(dx, dy, dz):
        return (
            lax.rem(cx + dx, N_X) * N_CORE + cc,
            lax.rem(cz + dz, N_Z) * N_Y + lax.rem(cy + dy, N_Y),
        )

    x_line = [around(dx, 0, 0) for dx in (2, 1, 3)]
    y_line = [around(0, dy, 0) for dy in (2, 1, 3)]
    z_near = [around(0, 0, 1), around(0, 0, N_Z - 1)]
    z_next = [around(0, 0, 2), around(0, 0, N_Z - 2)]

    barrier = pltpu.get_barrier_semaphore()
    near = [up_dev, down_dev, pair_dev] + x_line + y_line + z_near
    for dev in near:
        pl.semaphore_signal(barrier, inc=1, device_id=dev, device_id_type=MESH)
    feat_in.start()
    def occ_at(z):
        return occ_ref[:, pl.ds(z * PLANE, PLANE)].astype(F32)

    occ_in.wait()
    for n, z in enumerate((BS - 1, 0)):
        edges[n].wait()
        halo_send[0, n] = (edge_v[n].astype(F32) * occ_at(z)).astype(BF)

    def halo_copy(field, n):
        return pltpu.make_async_remote_copy(
            src_ref=halo_send.at[field, n],
            dst_ref=halo_recv.at[field, n],
            send_sem=halo_ssem.at[field, n],
            recv_sem=halo_rsem.at[field, n],
            device_id=(up_dev, down_dev)[n],
            device_id_type=MESH,
        )

    halos = [[halo_copy(field, n) for n in range(2)] for field in range(2)]
    def fill(s9, plane, layer, slot):
        lanes = pl.ds(pl.multiple_of(slot * PLANE, PLANE), PLANE)
        for k, moved in enumerate(spread(plane, x_iota)):
            s9[k * C : (k + 1) * C, lanes] = moved.astype(BF) * mask_v[layer, k]

    nb_in.wait()
    lane = lax.broadcasted_iota(jnp.int32, (C, PLANE), 1)
    x_iota = lane % BS
    y_iota = lane // BS
    for layer in range(3):
        flag = [jnp.where(nb_ref[0, 9 * layer + k] >= 0, 1.0, 0.0).astype(F32) for k in range(9)]
        for dy in (-1, 0, 1):
            y_out = y_iota == (BS - 1 if dy == 1 else 0 if dy == -1 else -1)
            for dx in (-1, 0, 1):
                x_out = x_iota == (BS - 1 if dx == 1 else 0 if dx == -1 else -1)

                def at(a, b):
                    return flag[3 * (a + 1) + b + 1]

                inner = jnp.where(x_out, at(0, dx), at(0, 0))
                outer = jnp.where(x_out, at(dy, dx), at(dy, 0))
                mask_v[layer, 3 * (dy + 1) + dx + 1] = jnp.where(y_out, outer, inner).astype(BF)


    def several(body, first, last):
        def step(n, carry):
            for m in range(UNROLL):
                body(first + n * UNROLL + m)
            return carry

        lax.fori_loop(0, (last - first) // UNROLL, step, 0)

    def own_plane(z):
        z0 = pl.multiple_of(z * PLANE, PLANE)
        occ = occ_ref[:, pl.ds(z0, PLANE)].astype(F32)
        live = feat_v[:, pl.ds(z0, PLANE)].astype(F32) * occ
        fill(s9f, live, 1, z + 1)
        ups = (cot_v[:, pl.ds(z0, PLANE)].astype(F32) * occ).astype(BF)
        for dz in range(3):
            u3[dz * C : (dz + 1) * C, pl.ds(pl.multiple_of((z + dz) * PLANE, PLANE), PLANE)] = ups

    part[24:30, :, C:128] = jnp.zeros((6, 32, C), F32)
    part[30:32] = jnp.zeros((2, 32, 128), F32)
    u3[0:C, V : V + PLANE] = jnp.zeros((C, PLANE), BF)
    u3[2 * C : 3 * C, PLANE : 2 * PLANE] = jnp.zeros((C, PLANE), BF)
    feat_in.wait()
    cot_in.wait()
    for n, z in enumerate((BS - 1, 0)):
        halo_send[1, n] = (cot_v[:, z * PLANE : (z + 1) * PLANE].astype(F32) * occ_at(z)).astype(BF)

    several(own_plane, 0, EARLY)
    pl.semaphore_wait(barrier, len(near))
    halos[0][0].start()
    halos[0][1].start()
    for dev in x_line + z_near:
        pl.semaphore_signal(round_sem.at[0], inc=1, device_id=dev, device_id_type=MESH)
    halos[1][0].start()
    halos[1][1].start()
    several(own_plane, EARLY, BS)


    def columns(t):
        return t * PLANE, min(PLANE, TAPS * C - t * PLANE)

    def chunk(t, n, r):
        return (2 * t + n // 128) * 6 + r

    nt = (((1,), (1,)), ((), ()))
    for t in range(3):
        base, width = columns(t)
        g = lax.dot_general(
            u3[:, PLANE : PLANE + V], s9f[base : base + width, PLANE : PLANE + V], nt,
            preferred_element_type=F32,
        )
        for n in range(0, width, 128):
            w = min(128, width - n)
            for r in range(6):
                part[chunk(t, n, r), :, 0:w] = g[32 * r : 32 * r + 32, n : n + w]

    pl.semaphore_wait(round_sem.at[0], len(x_line) + len(z_near))
    for dev in z_next:
        pl.semaphore_signal(round_sem.at[1], inc=1, device_id=dev, device_id_type=MESH)

    for n, layer in ((0, 0), (1, 2)):
        halos[0][n].wait_recv()
        slot = layer * (BS + 1) // 2
        fill(s9f, halo_recv[0, n].astype(F32), layer, slot)
        edge = u3[layer * C : layer * C + C, slot * PLANE : slot * PLANE + PLANE]
        for t in range(3):
            base, width = columns(t)
            g = lax.dot_general(
                edge, s9f[base : base + width, slot * PLANE : slot * PLANE + PLANE], nt,
                preferred_element_type=F32,
            )
            for m in range(0, width, 128):
                w = min(128, width - m)
                for h in range(2):
                    part[chunk(t, m, 2 * layer + h), :, 0:w] += g[32 * h : 32 * h + 32, m : m + w]

    rows = [slice(SUB * s, SUB * s + SUB) for s in range(SUBS)]

    def pair_copy(s):
        return pltpu.make_async_remote_copy(
            src_ref=part.at[pl.ds((1 - cc) * N_XY, N_XY), rows[s]],
            dst_ref=pair_recv.at[:, rows[s]],
            send_sem=pair_ssem.at[s],
            recv_sem=pair_rsem.at[s],
            device_id=pair_dev,
            device_id_type=MESH,
        )

    pairs = [pair_copy(s) for s in range(SUBS)]
    for copy in pairs:
        copy.start()

    def xy_copy(s, j):
        i, dev = xy_peer(j)
        return pltpu.make_async_remote_copy(
            src_ref=half.at[i, rows[s]],
            dst_ref=xy_recv.at[j, rows[s]],
            send_sem=xy_ssem.at[s, j],
            recv_sem=xy_rsem.at[s, j],
            device_id=dev,
            device_id_type=MESH,
        )

    xy_order = [10, 9, 11, 6, 7, 5, 14, 8, 2, 13, 3, 1, 15, 4, 12]
    xy_copies = []
    for s in range(SUBS):
        pairs[s].wait_recv()
        half[:, rows[s]] = part[pl.ds(cc * N_XY, N_XY), rows[s]] + pair_recv[:, rows[s]]
        xy_copies.append({j: xy_copy(s, j) for j in xy_order})
        for copy in xy_copies[s].values():
            copy.start()

    w_in.wait()
    for k in range(27):
        dz, j = k // 9, k % 9
        wf[dz * C : (dz + 1) * C, j * C : (j + 1) * C] = w_ref[k]
        wb[dz * C : (dz + 1) * C, j * C : (j + 1) * C] = jnp.transpose(w_ref[26 - k].astype(F32)).astype(BF)

    def convolve(weights, s9, dst):
        step = 6 * PLANE
        for n in range(0, EXT, step):
            products[:, n : n + step] = jnp.dot(
                weights[...], s9[:, n : n + step], preferred_element_type=F32
            )

        def combine(z, carry):
            z0 = pl.multiple_of(z * PLANE, PLANE)
            acc = products[0:C, pl.ds(z0, PLANE)]
            for dz in (1, 2):
                acc += products[dz * C : dz * C + C, pl.ds(pl.multiple_of(z0 + dz * PLANE, PLANE), PLANE)]
            dst[:, pl.ds(z0, PLANE)] = (acc * occ_ref[:, pl.ds(z0, PLANE)].astype(F32)).astype(BF)
            return carry

        lax.fori_loop(0, BS, combine, 0)

    convolve(wf, s9f, out_v)
    out_copy = pltpu.make_async_copy(out_v, out_hbm, out_sem.at[0])
    out_copy.start()

    def up_plane(z):
        z0 = pl.multiple_of((z + 1) * PLANE, PLANE)
        fill(s9u, u3[C : 2 * C, pl.ds(z0, PLANE)].astype(F32), 1, z + 1)

    several(up_plane, 0, UP_SPLIT)

    def z_copy(s, j):
        return pltpu.make_async_remote_copy(
            src_ref=own.at[rows[s]],
            dst_ref=z_recv.at[j, rows[s]],
            send_sem=z_ssem.at[s, j],
            recv_sem=z_rsem.at[s, j],
            device_id=z_peer(j),
            device_id_type=MESH,
        )

    pl.semaphore_wait(round_sem.at[1], len(z_next))
    z_order = [4, 3, 5, 2, 6, 1, 7]
    z_copies = []
    for s in range(SUBS):
        acc = half[xy, rows[s]]
        for j in xy_order:
            xy_copies[s][j].wait_recv()
        for j in xy_order:
            acc += xy_recv[j, rows[s]]
        own[rows[s]] = acc
        z_copies.append({j: z_copy(s, j) for j in z_order})
        for copy in z_copies[s].values():
            copy.start()

    halos[1][0].wait_recv()
    halos[1][1].wait_recv()
    fill(s9u, halo_recv[1, 0].astype(F32), 0, 0)
    fill(s9u, halo_recv[1, 1].astype(F32), 2, BS + 1)

    several(up_plane, UP_SPLIT, BS)
    convolve(wb, s9u, gin_v)
    gin_copy = pltpu.make_async_copy(gin_v, gin_hbm, out_sem.at[1])
    gin_copy.start()

    def back_copy(s, j):
        i, dev = xy_peer(j)
        return pltpu.make_async_remote_copy(
            src_ref=total.at[rows[s]],
            dst_ref=final.at[cc * N_XY + xy, rows[s]],
            send_sem=back_ssem.at[s, j],
            recv_sem=back_rsem.at[s, j],
            device_id=dev,
            device_id_type=MESH,
        )

    def forward(s, i):
        slot = final.at[cc * N_XY + i, rows[s]]
        copy = pltpu.make_async_remote_copy(
            src_ref=slot, dst_ref=slot, send_sem=on_ssem.at[s, i], recv_sem=on_rsem.at[s, i],
            device_id=pair_dev, device_id_type=MESH,
        )
        copy.start()
        return copy

    back_copies, forwards = [], []
    for s in range(SUBS):
        for j in z_order:
            z_copies[s][j].wait_recv()
        z_recv[0, rows[s]] = own[rows[s]]
        acc = z_recv[cz, rows[s]]
        for n in range(1, N_Z):
            acc += z_recv[lax.rem(cz + N_Z - n, N_Z), rows[s]]
        total[rows[s]] = acc
        back_copies.append({j: back_copy(s, j) for j in xy_order})
        for copy in back_copies[s].values():
            copy.start()
        final[cc * N_XY + xy, rows[s]] = acc
        chunk_ref[cc * N_XY + xy, rows[s]] = acc
        forwards.append(forward(s, xy))
    for s in range(SUBS):
        for j in reversed(xy_order):
            back_copies[s][j].wait_recv()
            i = lax.rem(xy + N_XY - j, N_XY)
            forwards.append(forward(s, i))
            chunk_ref[cc * N_XY + i, rows[s]] = final[cc * N_XY + i, rows[s]]
    for copy in forwards:
        copy.wait_recv()
    other = pl.ds((1 - cc) * N_XY, N_XY)
    chunk_ref[other] = final[other]

    for copy in pairs + forwards:
        copy.wait_send()
    for s in range(SUBS):
        for copies in (xy_copies[s], z_copies[s], back_copies[s]):
            for copy in copies.values():
                copy.wait_send()
    for field in range(2):
        for n in range(2):
            halos[field][n].wait_send()
    out_copy.wait()
    gin_copy.wait()


def deliver(out_ref, gin_ref, chunk_ref, out_hbm, gin_hbm, gw_hbm, gw_v, sems):
    copies = [
        pltpu.make_async_copy(out_ref, out_hbm, sems.at[0]),
        pltpu.make_async_copy(gin_ref, gin_hbm, sems.at[1]),
    ]
    for copy in copies:
        copy.start()
    for k in range(27):
        dz, j = k // 9, k % 9
        for h in range(2):
            gw_v[k, 32 * h : 32 * h + 32, :] = chunk_ref[(j // 2) * 6 + 2 * dz + h, :, (j % 2) * C : (j % 2 + 1) * C]
    gw_copy = pltpu.make_async_copy(gw_v, gw_hbm, sems.at[2])
    gw_copy.start()
    for copy in copies:
        copy.wait()
    gw_copy.wait()


def local(features, cotangent, weight, neighbours, occupancy):
    hbm = pl.BlockSpec(memory_space=pltpu.HBM)
    vmem = pl.BlockSpec(memory_space=pltpu.VMEM)
    anywhere = pl.BlockSpec(memory_space=pl.ANY)
    field = jax.ShapeDtypeStruct((C, V), BF)
    output, grad_input, chunks = pl.pallas_call(
        kernel,
        out_shape=(field, field, jax.ShapeDtypeStruct((32, 32, 128), F32)),
        in_specs=[hbm, hbm, hbm, hbm, hbm],
        out_specs=(anywhere, anywhere, vmem),
        scratch_shapes=[
            pltpu.VMEM((C, V), BF),
            pltpu.VMEM((C, V), BF),
            pltpu.VMEM((2, C, PLANE), BF),
            pltpu.VMEM((27, C, C), BF),
            pltpu.SMEM((1, 27), jnp.int32),
            pltpu.VMEM((1, V), jnp.int32),
            pltpu.VMEM((C, V), BF),
            pltpu.VMEM((C, V), BF),
            pltpu.VMEM((3 * C, EXT), F32),
            pltpu.VMEM((3, TAPS, C, PLANE), BF),
            pltpu.VMEM((TAPS * C, EXT), BF),
            pltpu.VMEM((TAPS * C, EXT), BF),
            pltpu.VMEM((3 * C, EXT), BF),
            pltpu.VMEM((3 * C, TAPS * C), BF),
            pltpu.VMEM((3 * C, TAPS * C), BF),
            pltpu.VMEM((2, 2, C, PLANE), BF),
            pltpu.VMEM((2, 2, C, PLANE), BF),
            pltpu.VMEM((32, 32, 128), F32),
            pltpu.VMEM((16, 32, 128), F32),
            pltpu.VMEM((16, 32, 128), F32),
            pltpu.VMEM((16, 32, 128), F32),
            pltpu.VMEM((32, 128), F32),
            pltpu.VMEM((8, 32, 128), F32),
            pltpu.VMEM((32, 128), F32),
            pltpu.VMEM((32, 32, 128), F32),
            pltpu.SemaphoreType.DMA((7,)),
            pltpu.SemaphoreType.DMA((3,)),
            pltpu.SemaphoreType.DMA((2, 2)),
            pltpu.SemaphoreType.DMA((2, 2)),
            pltpu.SemaphoreType.DMA((SUBS,)),
            pltpu.SemaphoreType.DMA((SUBS,)),
            pltpu.SemaphoreType.DMA((SUBS, N_XY)),
            pltpu.SemaphoreType.DMA((SUBS, N_XY)),
            pltpu.SemaphoreType.DMA((SUBS, N_Z)),
            pltpu.SemaphoreType.DMA((SUBS, N_Z)),
            pltpu.SemaphoreType.DMA((SUBS, N_XY)),
            pltpu.SemaphoreType.DMA((SUBS, N_XY)),
            pltpu.SemaphoreType.DMA((SUBS, N_XY)),
            pltpu.SemaphoreType.DMA((SUBS, N_XY)),
            pltpu.SemaphoreType.REGULAR((2,)),
        ],
        compiler_params=pltpu.CompilerParams(
            collective_id=0, has_side_effects=True, vmem_limit_bytes=40 * 2**20
        ),
    )(
        pltpu.with_memory_space_constraint(features.reshape(C, V), pltpu.HBM),
        pltpu.with_memory_space_constraint(cotangent.reshape(C, V), pltpu.HBM),
        pltpu.with_memory_space_constraint(weight, pltpu.HBM),
        pltpu.with_memory_space_constraint(neighbours.reshape(1, 27), pltpu.HBM),
        pltpu.with_memory_space_constraint(occupancy.reshape(1, V), pltpu.HBM),
    )
    output, grad_input, grad_weight = pl.pallas_call(
        deliver,
        out_shape=(field, field, jax.ShapeDtypeStruct((27, C, C), F32)),
        in_specs=[anywhere, anywhere, vmem],
        out_specs=(hbm, hbm, hbm),
        scratch_shapes=[
            pltpu.VMEM((27, C, C), F32),
            pltpu.SemaphoreType.DMA((3,)),
        ],
        compiler_params=pltpu.CompilerParams(vmem_limit_bytes=16 * 2**20),
    )(output, grad_input, chunks)
    return output.reshape(1, 1, C, V), grad_input.reshape(1, 1, C, V), grad_weight


def solution(mesh):
    in_specs = (
        P("scan", "brick", None, None),
        P("scan", "brick", None, None),
        P(),
        P("scan", "brick", None),
        P("scan", "brick", None),
    )
    out_specs = (P("scan", "brick", None, None), P("scan", "brick", None, None), P())
    return jax.shard_map(local, mesh=mesh, in_specs=in_specs, out_specs=out_specs, check_vma=False)
```

```python
import jax
import jax.numpy as jnp
from jax import lax
from jax.experimental import pallas as pl
from jax.experimental.pallas import tpu as pltpu
from jax.sharding import PartitionSpec as P

C = 64
BS = 16
PLANE = BS * BS
V = BS * PLANE
EXT = (BS + 2) * PLANE
TAPS = 9
BF = jnp.bfloat16
F32 = jnp.float32
MESH = pl.DeviceIdType.MESH
N_CORE, N_X, N_Y, N_Z = 2, 4, 4, 8
N_BRICK = N_Y * N_Z
N_XY = N_X * N_Y
UNROLL = 4
SUBS = 1
SUB = 32 // SUBS
UP_SPLIT = 16
GROUP = 2


def spread(plane, x_iota):
    left = jnp.where(x_iota == 0, pltpu.roll(plane, PLANE - 15, 1), pltpu.roll(plane, 1, 1))
    right = jnp.where(x_iota == BS - 1, pltpu.roll(plane, 15, 1), pltpu.roll(plane, PLANE - 1, 1))
    shifted = []
    for dy in (-1, 0, 1):
        for base in (left, plane, right):
            shifted.append(base if dy == 0 else pltpu.roll(base, (-dy * BS) % PLANE, 1))
    return shifted


def kernel(
    feat_hbm, cot_hbm, w_hbm, nb_hbm, occ_hbm,
    out_hbm, gin_hbm, chunk_ref,
    feat_v, cot_v, edge_v, w_ref, nb_ref, occ_ref, out_v, gin_v, products, partial, mask_v, s9f, s9u, u3, wf, wb,
    halo_send, halo_recv, part, pair_recv, half, xy_recv, own, z_recv, total, final,
    in_sem, out_sem, halo_ssem, halo_rsem, pair_ssem, pair_rsem, xy_ssem, xy_rsem, z_ssem, z_rsem, back_ssem, back_rsem, on_ssem, on_rsem, round_sem,
):
    scan = lax.axis_index("scan")
    brick = lax.axis_index("brick")
    cx, cc = scan // N_CORE, scan % N_CORE
    cz, cy = brick // N_Y, brick % N_Y
    xy = cx * N_Y + cy
    up_dev = (scan, lax.rem(brick + 1, N_BRICK))
    down_dev = (scan, lax.rem(brick + N_BRICK - 1, N_BRICK))
    pair_dev = (cx * N_CORE + 1 - cc, brick)

    def xy_peer(j):
        i = lax.rem(xy + j, N_XY)
        return i, ((i // N_Y) * N_CORE + cc, cz * N_Y + lax.rem(i, N_Y))

    def z_peer(j):
        return (scan, lax.rem(cz + j, N_Z) * N_Y + cy)

    def edge_in(hbm, n):
        lanes = pl.ds((BS - 1) * PLANE * (1 - n), PLANE)
        return pltpu.make_async_copy(hbm.at[:, lanes], edge_v.at[n], in_sem.at[5 + n])

    edges = [edge_in(feat_hbm, n) for n in range(2)]
    feat_in = pltpu.make_async_copy(feat_hbm, feat_v, in_sem.at[0])
    cot_in = pltpu.make_async_copy(cot_hbm, cot_v, in_sem.at[1])
    w_in = pltpu.make_async_copy(w_hbm, w_ref, in_sem.at[2])
    occ_in = pltpu.make_async_copy(occ_hbm, occ_ref, in_sem.at[3])
    nb_in = pltpu.make_async_copy(nb_hbm, nb_ref, in_sem.at[4])
    occ_in.start()
    edges[0].start()
    edges[1].start()

    cot_in.start()
    w_in.start()
    nb_in.start()

    def around(dx, dy, dz):
        return (
            lax.rem(cx + dx, N_X) * N_CORE + cc,
            lax.rem(cz + dz, N_Z) * N_Y + lax.rem(cy + dy, N_Y),
        )

    x_line = [around(dx, 0, 0) for dx in (2, 1, 3)]
    y_line = [around(0, dy, 0) for dy in (2, 1, 3)]
    z_near = [around(0, 0, 1), around(0, 0, N_Z - 1)]
    z_next = [around(0, 0, 2), around(0, 0, N_Z - 2)]

    barrier = pltpu.get_barrier_semaphore()
    near = [up_dev, down_dev, pair_dev] + x_line + y_line + z_near
    for dev in near:
        pl.semaphore_signal(barrier, inc=1, device_id=dev, device_id_type=MESH)
    feat_in.start()
    def occ_at(z):
        return occ_ref[:, pl.ds(z * PLANE, PLANE)].astype(F32)

    occ_in.wait()
    for n, z in enumerate((BS - 1, 0)):
        edges[n].wait()
        halo_send[0, n] = (edge_v[n].astype(F32) * occ_at(z)).astype(BF)

    def halo_copy(field, n):
        return pltpu.make_async_remote_copy(
            src_ref=halo_send.at[field, n],
            dst_ref=halo_recv.at[field, n],
            send_sem=halo_ssem.at[field, n],
            recv_sem=halo_rsem.at[field, n],
            device_id=(up_dev, down_dev)[n],
            device_id_type=MESH,
        )

    halos = [[halo_copy(field, n) for n in range(2)] for field in range(2)]
    def lane_of(plane):
        return plane * PLANE if isinstance(plane, int) else pl.multiple_of(plane * PLANE, PLANE)

    def fill(s9, plane, layer, slot):
        lanes = pl.ds(lane_of(slot), PLANE)
        for k, moved in enumerate(spread(plane, x_iota)):
            s9[k * C : (k + 1) * C, lanes] = moved.astype(BF) * mask_v[layer, k]

    nb_in.wait()
    lane = lax.broadcasted_iota(jnp.int32, (C, PLANE), 1)
    x_iota = lane % BS
    y_iota = lane // BS
    for layer in range(3):
        flag = [jnp.where(nb_ref[0, 9 * layer + k] >= 0, 1.0, 0.0).astype(F32) for k in range(9)]
        for dy in (-1, 0, 1):
            y_out = y_iota == (BS - 1 if dy == 1 else 0 if dy == -1 else -1)
            for dx in (-1, 0, 1):
                x_out = x_iota == (BS - 1 if dx == 1 else 0 if dx == -1 else -1)

                def at(a, b):
                    return flag[3 * (a + 1) + b + 1]

                inner = jnp.where(x_out, at(0, dx), at(0, 0))
                outer = jnp.where(x_out, at(dy, dx), at(dy, 0))
                mask_v[layer, 3 * (dy + 1) + dx + 1] = jnp.where(y_out, outer, inner).astype(BF)


    def several(body, first, last):
        def step(n, carry):
            for m in range(UNROLL):
                body(first + n * UNROLL + m)
            return carry

        lax.fori_loop(0, (last - first) // UNROLL, step, 0)

    def own_plane(z):
        z0 = lane_of(z)
        occ = occ_ref[:, pl.ds(z0, PLANE)].astype(F32)
        fill(s9f, feat_v[:, pl.ds(z0, PLANE)].astype(F32) * occ, 1, z + 1)

    def up_rows(z):
        z0 = lane_of(z)
        occ = occ_ref[:, pl.ds(z0, PLANE)].astype(F32)
        ups = (cot_v[:, pl.ds(z0, PLANE)].astype(F32) * occ).astype(BF)
        for dz in range(3):
            u3[dz * C : (dz + 1) * C, pl.ds(lane_of(z + dz), PLANE)] = ups

    part[24:30, :, C:128] = jnp.zeros((6, 32, C), F32)
    part[30:32] = jnp.zeros((2, 32, 128), F32)
    u3[0:C, V : V + PLANE] = jnp.zeros((C, PLANE), BF)
    u3[2 * C : 3 * C, PLANE : 2 * PLANE] = jnp.zeros((C, PLANE), BF)
    feat_in.wait()
    cot_in.wait()
    for n, z in enumerate((BS - 1, 0)):
        halo_send[1, n] = (cot_v[:, z * PLANE : (z + 1) * PLANE].astype(F32) * occ_at(z)).astype(BF)

    several(up_rows, 0, BS)
    for z in range(GROUP):
        own_plane(z)
    pl.semaphore_wait(barrier, len(near))
    halos[0][0].start()
    halos[0][1].start()
    for dev in x_line + z_near:
        pl.semaphore_signal(round_sem.at[0], inc=1, device_id=dev, device_id_type=MESH)
    halos[1][0].start()
    halos[1][1].start()


    def columns(t):
        return t * PLANE, min(PLANE, TAPS * C - t * PLANE)

    def chunk(t, n, r):
        return (2 * t + n // 128) * 6 + r

    nt = (((1,), (1,)), ((), ()))
    for first in range(0, BS, GROUP):
        lanes = slice((first + 1) * PLANE, (first + 1 + GROUP) * PLANE)
        for t in range(3):
            base, width = columns(t)
            g = lax.dot_general(
                u3[:, lanes], s9f[base : base + width, lanes], nt, preferred_element_type=F32
            )
            if first > 0:
                g += partial[:, base : base + width]
            if first + GROUP < BS:
                partial[:, base : base + width] = g
                continue
            for n in range(0, width, 128):
                w = min(128, width - n)
                for r in range(6):
                    part[chunk(t, n, r), :, 0:w] = g[32 * r : 32 * r + 32, n : n + w]
        for z in range(first + GROUP, min(first + 2 * GROUP, BS)):
            own_plane(z)

    pl.semaphore_wait(round_sem.at[0], len(x_line) + len(z_near))
    for dev in z_next:
        pl.semaphore_signal(round_sem.at[1], inc=1, device_id=dev, device_id_type=MESH)

    for n, layer in ((0, 0), (1, 2)):
        halos[0][n].wait_recv()
        slot = layer * (BS + 1) // 2
        fill(s9f, halo_recv[0, n].astype(F32), layer, slot)
        edge = u3[layer * C : layer * C + C, slot * PLANE : slot * PLANE + PLANE]
        for t in range(3):
            base, width = columns(t)
            g = lax.dot_general(
                edge, s9f[base : base + width, slot * PLANE : slot * PLANE + PLANE], nt,
                preferred_element_type=F32,
            )
            for m in range(0, width, 128):
                w = min(128, width - m)
                for h in range(2):
                    part[chunk(t, m, 2 * layer + h), :, 0:w] += g[32 * h : 32 * h + 32, m : m + w]

    rows = [slice(SUB * s, SUB * s + SUB) for s in range(SUBS)]

    def pair_copy(s):
        return pltpu.make_async_remote_copy(
            src_ref=part.at[pl.ds((1 - cc) * N_XY, N_XY), rows[s]],
            dst_ref=pair_recv.at[:, rows[s]],
            send_sem=pair_ssem.at[s],
            recv_sem=pair_rsem.at[s],
            device_id=pair_dev,
            device_id_type=MESH,
        )

    pairs = [pair_copy(s) for s in range(SUBS)]
    for copy in pairs:
        copy.start()

    def xy_copy(s, j):
        i, dev = xy_peer(j)
        return pltpu.make_async_remote_copy(
            src_ref=half.at[i, rows[s]],
            dst_ref=xy_recv.at[j, rows[s]],
            send_sem=xy_ssem.at[s, j],
            recv_sem=xy_rsem.at[s, j],
            device_id=dev,
            device_id_type=MESH,
        )

    xy_order = [10, 9, 11, 6, 7, 5, 14, 8, 2, 13, 3, 1, 15, 4, 12]
    xy_copies = []
    for s in range(SUBS):
        pairs[s].wait_recv()
        half[:, rows[s]] = part[pl.ds(cc * N_XY, N_XY), rows[s]] + pair_recv[:, rows[s]]
        xy_copies.append({j: xy_copy(s, j) for j in xy_order})
        for copy in xy_copies[s].values():
            copy.start()

    w_in.wait()
    for k in range(27):
        dz, j = k // 9, k % 9
        wf[dz * C : (dz + 1) * C, j * C : (j + 1) * C] = w_ref[k]
        wb[dz * C : (dz + 1) * C, j * C : (j + 1) * C] = jnp.transpose(w_ref[26 - k].astype(F32)).astype(BF)

    def convolve(weights, s9, dst):
        step = 6 * PLANE
        for n in range(0, EXT, step):
            products[:, n : n + step] = jnp.dot(
                weights[...], s9[:, n : n + step], preferred_element_type=F32
            )

        def combine(z, carry):
            z0 = pl.multiple_of(z * PLANE, PLANE)
            acc = products[0:C, pl.ds(z0, PLANE)]
            for dz in (1, 2):
                acc += products[dz * C : dz * C + C, pl.ds(pl.multiple_of(z0 + dz * PLANE, PLANE), PLANE)]
            dst[:, pl.ds(z0, PLANE)] = (acc * occ_ref[:, pl.ds(z0, PLANE)].astype(F32)).astype(BF)
            return carry

        lax.fori_loop(0, BS, combine, 0)

    convolve(wf, s9f, out_v)
    out_copy = pltpu.make_async_copy(out_v, out_hbm, out_sem.at[0])
    out_copy.start()

    def up_plane(z):
        z0 = pl.multiple_of((z + 1) * PLANE, PLANE)
        fill(s9u, u3[C : 2 * C, pl.ds(z0, PLANE)].astype(F32), 1, z + 1)

    several(up_plane, 0, UP_SPLIT)

    def z_copy(s, j):
        return pltpu.make_async_remote_copy(
            src_ref=own.at[rows[s]],
            dst_ref=z_recv.at[j, rows[s]],
            send_sem=z_ssem.at[s, j],
            recv_sem=z_rsem.at[s, j],
            device_id=z_peer(j),
            device_id_type=MESH,
        )

    pl.semaphore_wait(round_sem.at[1], len(z_next))
    z_order = [4, 3, 5, 2, 6, 1, 7]
    z_copies = []
    for s in range(SUBS):
        acc = half[xy, rows[s]]
        for j in xy_order:
            xy_copies[s][j].wait_recv()
        for j in xy_order:
            acc += xy_recv[j, rows[s]]
        own[rows[s]] = acc
        z_copies.append({j: z_copy(s, j) for j in z_order})
        for copy in z_copies[s].values():
            copy.start()

    halos[1][0].wait_recv()
    halos[1][1].wait_recv()
    fill(s9u, halo_recv[1, 0].astype(F32), 0, 0)
    fill(s9u, halo_recv[1, 1].astype(F32), 2, BS + 1)

    several(up_plane, UP_SPLIT, BS)
    convolve(wb, s9u, gin_v)
    gin_copy = pltpu.make_async_copy(gin_v, gin_hbm, out_sem.at[1])
    gin_copy.start()

    def back_copy(s, j):
        i, dev = xy_peer(j)
        return pltpu.make_async_remote_copy(
            src_ref=total.at[rows[s]],
            dst_ref=final.at[cc * N_XY + xy, rows[s]],
            send_sem=back_ssem.at[s, j],
            recv_sem=back_rsem.at[s, j],
            device_id=dev,
            device_id_type=MESH,
        )

    def forward(s, i):
        slot = final.at[cc * N_XY + i, rows[s]]
        copy = pltpu.make_async_remote_copy(
            src_ref=slot, dst_ref=slot, send_sem=on_ssem.at[s, i], recv_sem=on_rsem.at[s, i],
            device_id=pair_dev, device_id_type=MESH,
        )
        copy.start()
        return copy

    back_copies, forwards = [], []
    for s in range(SUBS):
        for j in z_order:
            z_copies[s][j].wait_recv()
        z_recv[0, rows[s]] = own[rows[s]]
        acc = z_recv[cz, rows[s]]
        for n in range(1, N_Z):
            acc += z_recv[lax.rem(cz + N_Z - n, N_Z), rows[s]]
        total[rows[s]] = acc
        back_copies.append({j: back_copy(s, j) for j in xy_order})
        for copy in back_copies[s].values():
            copy.start()
        final[cc * N_XY + xy, rows[s]] = acc
        chunk_ref[cc * N_XY + xy, rows[s]] = acc
        forwards.append(forward(s, xy))
    for s in range(SUBS):
        for j in reversed(xy_order):
            back_copies[s][j].wait_recv()
            i = lax.rem(xy + N_XY - j, N_XY)
            forwards.append(forward(s, i))
            chunk_ref[cc * N_XY + i, rows[s]] = final[cc * N_XY + i, rows[s]]
    for copy in forwards:
        copy.wait_recv()
    other = pl.ds((1 - cc) * N_XY, N_XY)
    chunk_ref[other] = final[other]

    for copy in pairs + forwards:
        copy.wait_send()
    for s in range(SUBS):
        for copies in (xy_copies[s], z_copies[s], back_copies[s]):
            for copy in copies.values():
                copy.wait_send()
    for field in range(2):
        for n in range(2):
            halos[field][n].wait_send()
    out_copy.wait()
    gin_copy.wait()


def deliver(out_ref, gin_ref, chunk_ref, out_hbm, gin_hbm, gw_hbm, gw_v, sems):
    copies = [
        pltpu.make_async_copy(out_ref, out_hbm, sems.at[0]),
        pltpu.make_async_copy(gin_ref, gin_hbm, sems.at[1]),
    ]
    for copy in copies:
        copy.start()
    for k in range(27):
        dz, j = k // 9, k % 9
        for h in range(2):
            gw_v[k, 32 * h : 32 * h + 32, :] = chunk_ref[(j // 2) * 6 + 2 * dz + h, :, (j % 2) * C : (j % 2 + 1) * C]
    gw_copy = pltpu.make_async_copy(gw_v, gw_hbm, sems.at[2])
    gw_copy.start()
    for copy in copies:
        copy.wait()
    gw_copy.wait()


def local(features, cotangent, weight, neighbours, occupancy):
    hbm = pl.BlockSpec(memory_space=pltpu.HBM)
    vmem = pl.BlockSpec(memory_space=pltpu.VMEM)
    anywhere = pl.BlockSpec(memory_space=pl.ANY)
    field = jax.ShapeDtypeStruct((C, V), BF)
    output, grad_input, chunks = pl.pallas_call(
        kernel,
        out_shape=(field, field, jax.ShapeDtypeStruct((32, 32, 128), F32)),
        in_specs=[hbm, hbm, hbm, hbm, hbm],
        out_specs=(anywhere, anywhere, vmem),
        scratch_shapes=[
            pltpu.VMEM((C, V), BF),
            pltpu.VMEM((C, V), BF),
            pltpu.VMEM((2, C, PLANE), BF),
            pltpu.VMEM((27, C, C), BF),
            pltpu.SMEM((1, 27), jnp.int32),
            pltpu.VMEM((1, V), jnp.int32),
            pltpu.VMEM((C, V), BF),
            pltpu.VMEM((C, V), BF),
            pltpu.VMEM((3 * C, EXT), F32),
            pltpu.VMEM((3 * C, TAPS * C), F32),
            pltpu.VMEM((3, TAPS, C, PLANE), BF),
            pltpu.VMEM((TAPS * C, EXT), BF),
            pltpu.VMEM((TAPS * C, EXT), BF),
            pltpu.VMEM((3 * C, EXT), BF),
            pltpu.VMEM((3 * C, TAPS * C), BF),
            pltpu.VMEM((3 * C, TAPS * C), BF),
            pltpu.VMEM((2, 2, C, PLANE), BF),
            pltpu.VMEM((2, 2, C, PLANE), BF),
            pltpu.VMEM((32, 32, 128), F32),
            pltpu.VMEM((16, 32, 128), F32),
            pltpu.VMEM((16, 32, 128), F32),
            pltpu.VMEM((16, 32, 128), F32),
            pltpu.VMEM((32, 128), F32),
            pltpu.VMEM((8, 32, 128), F32),
            pltpu.VMEM((32, 128), F32),
            pltpu.VMEM((32, 32, 128), F32),
            pltpu.SemaphoreType.DMA((7,)),
            pltpu.SemaphoreType.DMA((3,)),
            pltpu.SemaphoreType.DMA((2, 2)),
            pltpu.SemaphoreType.DMA((2, 2)),
            pltpu.SemaphoreType.DMA((SUBS,)),
            pltpu.SemaphoreType.DMA((SUBS,)),
            pltpu.SemaphoreType.DMA((SUBS, N_XY)),
            pltpu.SemaphoreType.DMA((SUBS, N_XY)),
            pltpu.SemaphoreType.DMA((SUBS, N_Z)),
            pltpu.SemaphoreType.DMA((SUBS, N_Z)),
            pltpu.SemaphoreType.DMA((SUBS, N_XY)),
            pltpu.SemaphoreType.DMA((SUBS, N_XY)),
            pltpu.SemaphoreType.DMA((SUBS, N_XY)),
            pltpu.SemaphoreType.DMA((SUBS, N_XY)),
            pltpu.SemaphoreType.REGULAR((2,)),
        ],
        compiler_params=pltpu.CompilerParams(
            collective_id=0, has_side_effects=True, vmem_limit_bytes=40 * 2**20
        ),
    )(
        pltpu.with_memory_space_constraint(features.reshape(C, V), pltpu.HBM),
        pltpu.with_memory_space_constraint(cotangent.reshape(C, V), pltpu.HBM),
        pltpu.with_memory_space_constraint(weight, pltpu.HBM),
        pltpu.with_memory_space_constraint(neighbours.reshape(1, 27), pltpu.HBM),
        pltpu.with_memory_space_constraint(occupancy.reshape(1, V), pltpu.HBM),
    )
    output, grad_input, grad_weight = pl.pallas_call(
        deliver,
        out_shape=(field, field, jax.ShapeDtypeStruct((27, C, C), F32)),
        in_specs=[anywhere, anywhere, vmem],
        out_specs=(hbm, hbm, hbm),
        scratch_shapes=[
            pltpu.VMEM((27, C, C), F32),
            pltpu.SemaphoreType.DMA((3,)),
        ],
        compiler_params=pltpu.CompilerParams(vmem_limit_bytes=16 * 2**20),
    )(output, grad_input, chunks)
    return output.reshape(1, 1, C, V), grad_input.reshape(1, 1, C, V), grad_weight


def solution(mesh):
    in_specs = (
        P("scan", "brick", None, None),
        P("scan", "brick", None, None),
        P(),
        P("scan", "brick", None),
        P("scan", "brick", None),
    )
    out_specs = (P("scan", "brick", None, None), P("scan", "brick", None, None), P())
    return jax.shard_map(local, mesh=mesh, in_specs=in_specs, out_specs=out_specs, check_vma=False)
```

```python
import functools

import jax
import jax.numpy as jnp
from jax import lax
from jax.experimental import pallas as pl
from jax.experimental.pallas import tpu as pltpu
from jax.sharding import PartitionSpec as P

C = 64
BS = 16
PLANE = BS * BS
V = BS * PLANE
EXT = (BS + 2) * PLANE
TAPS = 9
BF = jnp.bfloat16
F32 = jnp.float32
MESH = pl.DeviceIdType.MESH
N_CORE, N_X, N_Y, N_Z = 2, 4, 4, 8
N_BRICK = N_Y * N_Z
N_XY = N_X * N_Y
UNROLL = 4
SUBS = 1
SUB = 32 // SUBS
UP_SPLIT = 16
GROUP = 2


OWNERS = 14


def slot_of(chunk):
    return chunk if chunk < OWNERS else chunk - OWNERS + N_XY


def spread(plane, x_iota):
    left = jnp.where(x_iota == 0, pltpu.roll(plane, PLANE - 15, 1), pltpu.roll(plane, 1, 1))
    right = jnp.where(x_iota == BS - 1, pltpu.roll(plane, 15, 1), pltpu.roll(plane, PLANE - 1, 1))
    shifted = []
    for dy in (-1, 0, 1):
        for base in (left, plane, right):
            shifted.append(base if dy == 0 else pltpu.roll(base, (-dy * BS) % PLANE, 1))
    return shifted


def kernel(
    feat_hbm, cot_hbm, w_hbm, nb_hbm, occ_hbm,
    out_hbm, gin_hbm, chunk_ref,
    feat_v, cot_v, edge_v, w_ref, nb_ref, occ_ref, out_v, gin_v, products, partial, mask_v, s9f, s9u, u3, wf, wb,
    halo_send, halo_recv, part, pair_recv, half, xy_recv, own, z_recv, total, final,
    in_sem, out_sem, halo_ssem, halo_rsem, pair_ssem, pair_rsem, xy_ssem, xy_rsem, z_ssem, z_rsem, back_ssem, back_rsem, on_ssem, on_rsem, round_sem,
):
    scan = lax.axis_index("scan")
    brick = lax.axis_index("brick")
    cx, cc = scan // N_CORE, scan % N_CORE
    cz, cy = brick // N_Y, brick % N_Y
    xy = cx * N_Y + cy
    up_dev = (scan, lax.rem(brick + 1, N_BRICK))
    down_dev = (scan, lax.rem(brick + N_BRICK - 1, N_BRICK))
    pair_dev = (cx * N_CORE + 1 - cc, brick)

    def xy_peer(j):
        i = lax.rem(xy + j, N_XY)
        return i, ((i // N_Y) * N_CORE + cc, cz * N_Y + lax.rem(i, N_Y))

    def z_peer(j):
        return (scan, lax.rem(cz + j, N_Z) * N_Y + cy)

    def edge_in(hbm, n):
        lanes = pl.ds((BS - 1) * PLANE * (1 - n), PLANE)
        return pltpu.make_async_copy(hbm.at[:, lanes], edge_v.at[n], in_sem.at[5 + n])

    edges = [edge_in(feat_hbm, n) for n in range(2)]
    feat_in = pltpu.make_async_copy(feat_hbm, feat_v, in_sem.at[0])
    cot_in = pltpu.make_async_copy(cot_hbm, cot_v, in_sem.at[1])
    w_in = pltpu.make_async_copy(w_hbm, w_ref, in_sem.at[2])
    occ_in = pltpu.make_async_copy(occ_hbm, occ_ref, in_sem.at[3])
    nb_in = pltpu.make_async_copy(nb_hbm, nb_ref, in_sem.at[4])
    occ_in.start()
    edges[0].start()
    edges[1].start()

    cot_in.start()
    w_in.start()
    nb_in.start()

    def around(dx, dy, dz):
        return (
            lax.rem(cx + dx, N_X) * N_CORE + cc,
            lax.rem(cz + dz, N_Z) * N_Y + lax.rem(cy + dy, N_Y),
        )

    x_line = [around(dx, 0, 0) for dx in (2, 1, 3)]
    y_line = [around(0, dy, 0) for dy in (2, 1, 3)]
    z_near = [around(0, 0, 1), around(0, 0, N_Z - 1)]
    z_next = [around(0, 0, 2), around(0, 0, N_Z - 2)]

    barrier = pltpu.get_barrier_semaphore()
    near = [up_dev, down_dev, pair_dev] + x_line + y_line + z_near
    for dev in near:
        pl.semaphore_signal(barrier, inc=1, device_id=dev, device_id_type=MESH)
    feat_in.start()
    def occ_at(z):
        return occ_ref[:, pl.ds(z * PLANE, PLANE)].astype(F32)

    occ_in.wait()
    for n, z in enumerate((BS - 1, 0)):
        edges[n].wait()
        halo_send[0, n] = (edge_v[n].astype(F32) * occ_at(z)).astype(BF)

    def halo_copy(field, n):
        return pltpu.make_async_remote_copy(
            src_ref=halo_send.at[field, n],
            dst_ref=halo_recv.at[field, n],
            send_sem=halo_ssem.at[field, n],
            recv_sem=halo_rsem.at[field, n],
            device_id=(up_dev, down_dev)[n],
            device_id_type=MESH,
        )

    halos = [[halo_copy(field, n) for n in range(2)] for field in range(2)]
    def lane_of(plane):
        return plane * PLANE if isinstance(plane, int) else pl.multiple_of(plane * PLANE, PLANE)

    def fill(s9, plane, layer, slot):
        lanes = pl.ds(lane_of(slot), PLANE)
        for k, moved in enumerate(spread(plane, x_iota)):
            s9[k * C : (k + 1) * C, lanes] = moved.astype(BF) * mask_v[layer, k]

    nb_in.wait()
    lane = lax.broadcasted_iota(jnp.int32, (C, PLANE), 1)
    x_iota = lane % BS
    y_iota = lane // BS
    for layer in range(3):
        flag = [jnp.where(nb_ref[0, 9 * layer + k] >= 0, 1.0, 0.0).astype(F32) for k in range(9)]
        for dy in (-1, 0, 1):
            y_out = y_iota == (BS - 1 if dy == 1 else 0 if dy == -1 else -1)
            for dx in (-1, 0, 1):
                x_out = x_iota == (BS - 1 if dx == 1 else 0 if dx == -1 else -1)

                def at(a, b):
                    return flag[3 * (a + 1) + b + 1]

                inner = jnp.where(x_out, at(0, dx), at(0, 0))
                outer = jnp.where(x_out, at(dy, dx), at(dy, 0))
                mask_v[layer, 3 * (dy + 1) + dx + 1] = jnp.where(y_out, outer, inner).astype(BF)


    def several(body, first, last):
        def step(n, carry):
            for m in range(UNROLL):
                body(first + n * UNROLL + m)
            return carry

        lax.fori_loop(0, (last - first) // UNROLL, step, 0)

    def own_plane(z):
        z0 = lane_of(z)
        occ = occ_ref[:, pl.ds(z0, PLANE)].astype(F32)
        fill(s9f, feat_v[:, pl.ds(z0, PLANE)].astype(F32) * occ, 1, z + 1)

    def up_rows(z):
        z0 = lane_of(z)
        occ = occ_ref[:, pl.ds(z0, PLANE)].astype(F32)
        ups = (cot_v[:, pl.ds(z0, PLANE)].astype(F32) * occ).astype(BF)
        for dz in range(3):
            u3[dz * C : (dz + 1) * C, pl.ds(lane_of(z + dz), PLANE)] = ups

    for n in (14, 15, 29, 30, 31):
        part[n] = jnp.zeros((32, 128), F32)
    u3[0:C, V : V + PLANE] = jnp.zeros((C, PLANE), BF)
    u3[2 * C : 3 * C, PLANE : 2 * PLANE] = jnp.zeros((C, PLANE), BF)
    feat_in.wait()
    cot_in.wait()
    for n, z in enumerate((BS - 1, 0)):
        halo_send[1, n] = (cot_v[:, z * PLANE : (z + 1) * PLANE].astype(F32) * occ_at(z)).astype(BF)

    several(up_rows, 0, BS)
    for z in range(GROUP):
        own_plane(z)
    pl.semaphore_wait(barrier, len(near))
    halos[0][0].start()
    halos[0][1].start()
    for dev in x_line + z_near:
        pl.semaphore_signal(round_sem.at[0], inc=1, device_id=dev, device_id_type=MESH)
    halos[1][0].start()
    halos[1][1].start()


    def columns(t):
        return t * PLANE, min(PLANE, TAPS * C - t * PLANE)

    def place(t, n, r):
        if t < 2:
            return slot_of((2 * t + n // 128) * 6 + r), slice(0, 128)
        return slot_of(24 + r // 2), slice(C * (r % 2), C * (r % 2) + C)

    nt = (((1,), (1,)), ((), ()))
    for first in range(0, BS, GROUP):
        lanes = slice((first + 1) * PLANE, (first + 1 + GROUP) * PLANE)
        for t in range(3):
            base, width = columns(t)
            g = lax.dot_general(
                u3[:, lanes], s9f[base : base + width, lanes], nt, preferred_element_type=F32
            )
            if first > 0:
                g += partial[:, base : base + width]
            if first + GROUP < BS:
                partial[:, base : base + width] = g
                continue
            for n in range(0, width, 128):
                w = min(128, width - n)
                for r in range(6):
                    at, cols = place(t, n, r)
                    part[at, :, cols] = g[32 * r : 32 * r + 32, n : n + w]
        for z in range(first + GROUP, min(first + 2 * GROUP, BS)):
            own_plane(z)

    pl.semaphore_wait(round_sem.at[0], len(x_line) + len(z_near))
    for dev in z_next:
        pl.semaphore_signal(round_sem.at[1], inc=1, device_id=dev, device_id_type=MESH)

    for n, layer in ((0, 0), (1, 2)):
        halos[0][n].wait_recv()
        slot = layer * (BS + 1) // 2
        fill(s9f, halo_recv[0, n].astype(F32), layer, slot)
        edge = u3[layer * C : layer * C + C, slot * PLANE : slot * PLANE + PLANE]
        for t in range(3):
            base, width = columns(t)
            g = lax.dot_general(
                edge, s9f[base : base + width, slot * PLANE : slot * PLANE + PLANE], nt,
                preferred_element_type=F32,
            )
            for m in range(0, width, 128):
                w = min(128, width - m)
                for h in range(2):
                    at, cols = place(t, m, 2 * layer + h)
                    part[at, :, cols] += g[32 * h : 32 * h + 32, m : m + w]

    rows = [slice(SUB * s, SUB * s + SUB) for s in range(SUBS)]

    def pair_copy(s):
        return pltpu.make_async_remote_copy(
            src_ref=part.at[pl.ds((1 - cc) * N_XY, OWNERS), rows[s]],
            dst_ref=pair_recv.at[0:OWNERS, rows[s]],
            send_sem=pair_ssem.at[s],
            recv_sem=pair_rsem.at[s],
            device_id=pair_dev,
            device_id_type=MESH,
        )

    pairs = [pair_copy(s) for s in range(SUBS)]
    for copy in pairs:
        copy.start()

    def xy_copy(s, j):
        i, dev = xy_peer(j)
        return pltpu.make_async_remote_copy(
            src_ref=half.at[i, rows[s]],
            dst_ref=xy_recv.at[j, rows[s]],
            send_sem=xy_ssem.at[s, j],
            recv_sem=xy_rsem.at[s, j],
            device_id=dev,
            device_id_type=MESH,
        )

    xy_order = [10, 9, 11, 6, 7, 5, 14, 8, 2, 13, 3, 1, 15, 4, 12]
    xy_copies = []
    for s in range(SUBS):
        pairs[s].wait_recv()
        half[0:OWNERS, rows[s]] = part[pl.ds(cc * N_XY, OWNERS), rows[s]] + pair_recv[0:OWNERS, rows[s]]
        xy_copies.append({j: xy_copy(s, j) for j in xy_order})
        for j in xy_order:
            pl.when(lax.rem(xy + j, N_XY) < OWNERS)(xy_copies[s][j].start)

    w_in.wait()
    for k in range(27):
        dz, j = k // 9, k % 9
        wf[dz * C : (dz + 1) * C, j * C : (j + 1) * C] = w_ref[k]
        wb[dz * C : (dz + 1) * C, j * C : (j + 1) * C] = jnp.transpose(w_ref[26 - k].astype(F32)).astype(BF)

    def convolve(weights, s9, dst):
        step = 6 * PLANE
        for n in range(0, EXT, step):
            products[:, n : n + step] = jnp.dot(
                weights[...], s9[:, n : n + step], preferred_element_type=F32
            )

        def combine(z, carry):
            z0 = pl.multiple_of(z * PLANE, PLANE)
            acc = products[0:C, pl.ds(z0, PLANE)]
            for dz in (1, 2):
                acc += products[dz * C : dz * C + C, pl.ds(pl.multiple_of(z0 + dz * PLANE, PLANE), PLANE)]
            dst[:, pl.ds(z0, PLANE)] = (acc * occ_ref[:, pl.ds(z0, PLANE)].astype(F32)).astype(BF)
            return carry

        lax.fori_loop(0, BS, combine, 0)

    convolve(wf, s9f, out_v)
    out_copy = pltpu.make_async_copy(out_v, out_hbm, out_sem.at[0])
    out_copy.start()

    def up_plane(z):
        z0 = pl.multiple_of((z + 1) * PLANE, PLANE)
        fill(s9u, u3[C : 2 * C, pl.ds(z0, PLANE)].astype(F32), 1, z + 1)

    several(up_plane, 0, UP_SPLIT)

    def z_copy(s, j):
        return pltpu.make_async_remote_copy(
            src_ref=own.at[rows[s]],
            dst_ref=z_recv.at[j, rows[s]],
            send_sem=z_ssem.at[s, j],
            recv_sem=z_rsem.at[s, j],
            device_id=z_peer(j),
            device_id_type=MESH,
        )

    pl.semaphore_wait(round_sem.at[1], len(z_next))
    z_order = [4, 3, 5, 2, 6, 1, 7]
    owner = xy < OWNERS
    z_copies = [{j: z_copy(s, j) for j in z_order} for s in range(SUBS)]

    @pl.when(owner)
    def _():
        for s in range(SUBS):
            acc = half[xy, rows[s]]
            for j in xy_order:
                xy_copies[s][j].wait_recv()
            for j in xy_order:
                acc += xy_recv[j, rows[s]]
            own[rows[s]] = acc
            for copy in z_copies[s].values():
                copy.start()

    halos[1][0].wait_recv()
    halos[1][1].wait_recv()
    fill(s9u, halo_recv[1, 0].astype(F32), 0, 0)
    fill(s9u, halo_recv[1, 1].astype(F32), 2, BS + 1)

    several(up_plane, UP_SPLIT, BS)
    convolve(wb, s9u, gin_v)
    gin_copy = pltpu.make_async_copy(gin_v, gin_hbm, out_sem.at[1])
    gin_copy.start()

    def back_copy(s, j):
        i, dev = xy_peer(j)
        return pltpu.make_async_remote_copy(
            src_ref=total.at[rows[s]],
            dst_ref=final.at[cc * N_XY + xy, rows[s]],
            send_sem=back_ssem.at[s, j],
            recv_sem=back_rsem.at[s, j],
            device_id=dev,
            device_id_type=MESH,
        )

    def forward(s, i):
        slot = final.at[cc * N_XY + i, rows[s]]
        copy = pltpu.make_async_remote_copy(
            src_ref=slot, dst_ref=slot, send_sem=on_ssem.at[s, i], recv_sem=on_rsem.at[s, i],
            device_id=pair_dev, device_id_type=MESH,
        )
        return copy

    back_copies = [{j: back_copy(s, j) for j in xy_order} for s in range(SUBS)]
    forwards = [{j: forward(s, lax.rem(xy + N_XY - j, N_XY)) for j in range(N_XY)} for s in range(SUBS)]

    @pl.when(owner)
    def _():
        for s in range(SUBS):
            for j in z_order:
                z_copies[s][j].wait_recv()
            z_recv[0, rows[s]] = own[rows[s]]
            acc = z_recv[cz, rows[s]]
            for n in range(1, N_Z):
                acc += z_recv[lax.rem(cz + N_Z - n, N_Z), rows[s]]
            total[rows[s]] = acc
            for copy in back_copies[s].values():
                copy.start()
            final[cc * N_XY + xy, rows[s]] = acc
            chunk_ref[cc * N_XY + xy, rows[s]] = acc
            forwards[s][0].start()

    def sender(j):
        return lax.rem(xy + N_XY - j, N_XY)

    def pass_on(s, j):
        back_copies[s][j].wait_recv()
        forwards[s][j].start()
        chunk_ref[cc * N_XY + sender(j), rows[s]] = final[cc * N_XY + sender(j), rows[s]]

    for s in range(SUBS):
        for j in reversed(xy_order):
            pl.when(sender(j) < OWNERS)(functools.partial(pass_on, s, j))
    for s in range(SUBS):
        for j in range(N_XY):
            pl.when(sender(j) < OWNERS)(forwards[s][j].wait_recv)
    other = pl.ds((1 - cc) * N_XY, OWNERS)
    chunk_ref[other] = final[other]

    for s in range(SUBS):
        pairs[s].wait_send()
        for j in xy_order:
            pl.when(lax.rem(xy + j, N_XY) < OWNERS)(xy_copies[s][j].wait_send)
        for j in range(N_XY):
            pl.when(sender(j) < OWNERS)(forwards[s][j].wait_send)

    @pl.when(owner)
    def _():
        for s in range(SUBS):
            for copies in (z_copies[s], back_copies[s]):
                for copy in copies.values():
                    copy.wait_send()

    for field in range(2):
        for n in range(2):
            halos[field][n].wait_send()
    out_copy.wait()
    gin_copy.wait()


def deliver(out_ref, gin_ref, chunk_ref, out_hbm, gin_hbm, gw_hbm, gw_v, sems):
    copies = [
        pltpu.make_async_copy(out_ref, out_hbm, sems.at[0]),
        pltpu.make_async_copy(gin_ref, gin_hbm, sems.at[1]),
    ]
    for copy in copies:
        copy.start()
    for k in range(27):
        dz, j = k // 9, k % 9
        for h in range(2):
            if j < 8:
                at, half = slot_of((j // 2) * 6 + 2 * dz + h), j % 2
            else:
                at, half = slot_of(24 + dz), h
            gw_v[k, 32 * h : 32 * h + 32, :] = chunk_ref[at, :, C * half : C * half + C]
    gw_copy = pltpu.make_async_copy(gw_v, gw_hbm, sems.at[2])
    gw_copy.start()
    for copy in copies:
        copy.wait()
    gw_copy.wait()


def local(features, cotangent, weight, neighbours, occupancy):
    hbm = pl.BlockSpec(memory_space=pltpu.HBM)
    vmem = pl.BlockSpec(memory_space=pltpu.VMEM)
    anywhere = pl.BlockSpec(memory_space=pl.ANY)
    field = jax.ShapeDtypeStruct((C, V), BF)
    output, grad_input, chunks = pl.pallas_call(
        kernel,
        out_shape=(field, field, jax.ShapeDtypeStruct((32, 32, 128), F32)),
        in_specs=[hbm, hbm, hbm, hbm, hbm],
        out_specs=(anywhere, anywhere, vmem),
        scratch_shapes=[
            pltpu.VMEM((C, V), BF),
            pltpu.VMEM((C, V), BF),
            pltpu.VMEM((2, C, PLANE), BF),
            pltpu.VMEM((27, C, C), BF),
            pltpu.SMEM((1, 27), jnp.int32),
            pltpu.VMEM((1, V), jnp.int32),
            pltpu.VMEM((C, V), BF),
            pltpu.VMEM((C, V), BF),
            pltpu.VMEM((3 * C, EXT), F32),
            pltpu.VMEM((3 * C, TAPS * C), F32),
            pltpu.VMEM((3, TAPS, C, PLANE), BF),
            pltpu.VMEM((TAPS * C, EXT), BF),
            pltpu.VMEM((TAPS * C, EXT), BF),
            pltpu.VMEM((3 * C, EXT), BF),
            pltpu.VMEM((3 * C, TAPS * C), BF),
            pltpu.VMEM((3 * C, TAPS * C), BF),
            pltpu.VMEM((2, 2, C, PLANE), BF),
            pltpu.VMEM((2, 2, C, PLANE), BF),
            pltpu.VMEM((32, 32, 128), F32),
            pltpu.VMEM((16, 32, 128), F32),
            pltpu.VMEM((16, 32, 128), F32),
            pltpu.VMEM((16, 32, 128), F32),
            pltpu.VMEM((32, 128), F32),
            pltpu.VMEM((8, 32, 128), F32),
            pltpu.VMEM((32, 128), F32),
            pltpu.VMEM((32, 32, 128), F32),
            pltpu.SemaphoreType.DMA((7,)),
            pltpu.SemaphoreType.DMA((3,)),
            pltpu.SemaphoreType.DMA((2, 2)),
            pltpu.SemaphoreType.DMA((2, 2)),
            pltpu.SemaphoreType.DMA((SUBS,)),
            pltpu.SemaphoreType.DMA((SUBS,)),
            pltpu.SemaphoreType.DMA((SUBS, N_XY)),
            pltpu.SemaphoreType.DMA((SUBS, N_XY)),
            pltpu.SemaphoreType.DMA((SUBS, N_Z)),
            pltpu.SemaphoreType.DMA((SUBS, N_Z)),
            pltpu.SemaphoreType.DMA((SUBS, N_XY)),
            pltpu.SemaphoreType.DMA((SUBS, N_XY)),
            pltpu.SemaphoreType.DMA((SUBS, N_XY)),
            pltpu.SemaphoreType.DMA((SUBS, N_XY)),
            pltpu.SemaphoreType.REGULAR((2,)),
        ],
        compiler_params=pltpu.CompilerParams(
            collective_id=0, has_side_effects=True, vmem_limit_bytes=40 * 2**20
        ),
    )(
        pltpu.with_memory_space_constraint(features.reshape(C, V), pltpu.HBM),
        pltpu.with_memory_space_constraint(cotangent.reshape(C, V), pltpu.HBM),
        pltpu.with_memory_space_constraint(weight, pltpu.HBM),
        pltpu.with_memory_space_constraint(neighbours.reshape(1, 27), pltpu.HBM),
        pltpu.with_memory_space_constraint(occupancy.reshape(1, V), pltpu.HBM),
    )
    output, grad_input, grad_weight = pl.pallas_call(
        deliver,
        out_shape=(field, field, jax.ShapeDtypeStruct((27, C, C), F32)),
        in_specs=[anywhere, anywhere, vmem],
        out_specs=(hbm, hbm, hbm),
        scratch_shapes=[
            pltpu.VMEM((27, C, C), F32),
            pltpu.SemaphoreType.DMA((3,)),
        ],
        compiler_params=pltpu.CompilerParams(vmem_limit_bytes=16 * 2**20),
    )(output, grad_input, chunks)
    return output.reshape(1, 1, C, V), grad_input.reshape(1, 1, C, V), grad_weight


def solution(mesh):
    in_specs = (
        P("scan", "brick", None, None),
        P("scan", "brick", None, None),
        P(),
        P("scan", "brick", None),
        P("scan", "brick", None),
    )
    out_specs = (P("scan", "brick", None, None), P("scan", "brick", None, None), P())
    return jax.shard_map(local, mesh=mesh, in_specs=in_specs, out_specs=out_specs, check_vma=False)
```

```python
import functools

import jax
import jax.numpy as jnp
from jax import lax
from jax.experimental import pallas as pl
from jax.experimental.pallas import tpu as pltpu
from jax.sharding import PartitionSpec as P

C = 64
BS = 16
PLANE = BS * BS
V = BS * PLANE
EXT = (BS + 2) * PLANE
TAPS = 9
BF = jnp.bfloat16
F32 = jnp.float32
MESH = pl.DeviceIdType.MESH
N_CORE, N_X, N_Y, N_Z = 2, 4, 4, 8
N_BRICK = N_Y * N_Z
N_XY = N_X * N_Y
UNROLL = 4
SUBS = 1
SUB = 32 // SUBS
UP_SPLIT = 16
GROUP = 2


OWNERS = 14


def slot_of(chunk):
    return chunk if chunk < OWNERS else chunk - OWNERS + N_XY


def spread(plane, x_iota):
    left = jnp.where(x_iota == 0, pltpu.roll(plane, PLANE - 15, 1), pltpu.roll(plane, 1, 1))
    right = jnp.where(x_iota == BS - 1, pltpu.roll(plane, 15, 1), pltpu.roll(plane, PLANE - 1, 1))
    shifted = []
    for dy in (-1, 0, 1):
        for base in (left, plane, right):
            shifted.append(base if dy == 0 else pltpu.roll(base, (-dy * BS) % PLANE, 1))
    return shifted


def kernel(
    feat_hbm, cot_hbm, w_hbm, nb_hbm, occ_hbm,
    out_hbm, gin_hbm, chunk_ref,
    feat_v, cot_v, edge_v, w_ref, nb_ref, occ_ref, out_v, gin_v, products, partial, mask_v, s9f, s9u, u3, wf, wb,
    halo_send, halo_recv, part, pair_recv, half, xy_recv, own, z_recv, total, final,
    in_sem, out_sem, halo_ssem, halo_rsem, pair_ssem, pair_rsem, xy_ssem, xy_rsem, z_ssem, z_rsem, back_ssem, back_rsem, on_ssem, on_rsem, round_sem,
):
    scan = lax.axis_index("scan")
    brick = lax.axis_index("brick")
    cx, cc = scan // N_CORE, scan % N_CORE
    cz, cy = brick // N_Y, brick % N_Y
    xy = cx * N_Y + cy
    up_dev = (scan, lax.rem(brick + 1, N_BRICK))
    down_dev = (scan, lax.rem(brick + N_BRICK - 1, N_BRICK))
    pair_dev = (cx * N_CORE + 1 - cc, brick)

    def xy_peer(j):
        i = lax.rem(xy + j, N_XY)
        return i, ((i // N_Y) * N_CORE + cc, cz * N_Y + lax.rem(i, N_Y))

    def z_peer(j):
        return (scan, lax.rem(cz + j, N_Z) * N_Y + cy)

    def edge_in(hbm, n):
        lanes = pl.ds((BS - 1) * PLANE * (1 - n), PLANE)
        return pltpu.make_async_copy(hbm.at[:, lanes], edge_v.at[n], in_sem.at[5 + n])

    edges = [edge_in(feat_hbm, n) for n in range(2)]
    feat_in = pltpu.make_async_copy(feat_hbm, feat_v, in_sem.at[0])
    cot_in = pltpu.make_async_copy(cot_hbm, cot_v, in_sem.at[1])
    w_in = pltpu.make_async_copy(w_hbm, w_ref, in_sem.at[2])
    occ_in = pltpu.make_async_copy(occ_hbm, occ_ref, in_sem.at[3])
    nb_in = pltpu.make_async_copy(nb_hbm, nb_ref, in_sem.at[4])
    occ_in.start()
    edges[0].start()
    edges[1].start()

    cot_in.start()
    w_in.start()
    nb_in.start()

    def around(dx, dy, dz):
        return (
            lax.rem(cx + dx, N_X) * N_CORE + cc,
            lax.rem(cz + dz, N_Z) * N_Y + lax.rem(cy + dy, N_Y),
        )

    x_line = [around(dx, 0, 0) for dx in (2, 1, 3)]
    y_line = [around(0, dy, 0) for dy in (2, 1, 3)]
    z_near = [around(0, 0, 1), around(0, 0, N_Z - 1)]
    z_next = [around(0, 0, 2), around(0, 0, N_Z - 2)]

    barrier = pltpu.get_barrier_semaphore()
    near = [up_dev, down_dev, pair_dev] + x_line + y_line + z_near
    for dev in near:
        pl.semaphore_signal(barrier, inc=1, device_id=dev, device_id_type=MESH)
    feat_in.start()
    def occ_at(z):
        return occ_ref[:, pl.ds(z * PLANE, PLANE)].astype(F32)

    occ_in.wait()
    for n, z in enumerate((BS - 1, 0)):
        edges[n].wait()
        halo_send[0, n] = (edge_v[n].astype(F32) * occ_at(z)).astype(BF)

    def halo_copy(field, n):
        return pltpu.make_async_remote_copy(
            src_ref=halo_send.at[field, n],
            dst_ref=halo_recv.at[field, n],
            send_sem=halo_ssem.at[field, n],
            recv_sem=halo_rsem.at[field, n],
            device_id=(up_dev, down_dev)[n],
            device_id_type=MESH,
        )

    halos = [[halo_copy(field, n) for n in range(2)] for field in range(2)]
    def lane_of(plane):
        return plane * PLANE if isinstance(plane, int) else pl.multiple_of(plane * PLANE, PLANE)

    def fill(s9, plane, layer, slot):
        lanes = pl.ds(lane_of(slot), PLANE)
        for k, moved in enumerate(spread(plane, x_iota)):
            s9[k * C : (k + 1) * C, lanes] = moved.astype(BF) * mask_v[layer, k]

    nb_in.wait()
    lane = lax.broadcasted_iota(jnp.int32, (C, PLANE), 1)
    x_iota = lane % BS
    y_iota = lane // BS
    for layer in range(3):
        flag = [jnp.where(nb_ref[0, 9 * layer + k] >= 0, 1.0, 0.0).astype(F32) for k in range(9)]
        for dy in (-1, 0, 1):
            y_out = y_iota == (BS - 1 if dy == 1 else 0 if dy == -1 else -1)
            for dx in (-1, 0, 1):
                x_out = x_iota == (BS - 1 if dx == 1 else 0 if dx == -1 else -1)

                def at(a, b):
                    return flag[3 * (a + 1) + b + 1]

                inner = jnp.where(x_out, at(0, dx), at(0, 0))
                outer = jnp.where(x_out, at(dy, dx), at(dy, 0))
                mask_v[layer, 3 * (dy + 1) + dx + 1] = jnp.where(y_out, outer, inner).astype(BF)


    def several(body, first, last):
        def step(n, carry):
            for m in range(UNROLL):
                body(first + n * UNROLL + m)
            return carry

        lax.fori_loop(0, (last - first) // UNROLL, step, 0)

    def own_plane(z):
        z0 = lane_of(z)
        occ = occ_ref[:, pl.ds(z0, PLANE)].astype(F32)
        fill(s9f, feat_v[:, pl.ds(z0, PLANE)].astype(F32) * occ, 1, z + 1)

    def up_rows(z):
        z0 = lane_of(z)
        occ = occ_ref[:, pl.ds(z0, PLANE)].astype(F32)
        ups = (cot_v[:, pl.ds(z0, PLANE)].astype(F32) * occ).astype(BF)
        for dz in range(3):
            u3[dz * C : (dz + 1) * C, pl.ds(lane_of(z + dz), PLANE)] = ups

    for n in (14, 15, 29, 30, 31):
        part[n] = jnp.zeros((32, 128), F32)
    u3[0:C, V : V + PLANE] = jnp.zeros((C, PLANE), BF)
    u3[2 * C : 3 * C, PLANE : 2 * PLANE] = jnp.zeros((C, PLANE), BF)
    feat_in.wait()
    cot_in.wait()
    for n, z in enumerate((BS - 1, 0)):
        halo_send[1, n] = (cot_v[:, z * PLANE : (z + 1) * PLANE].astype(F32) * occ_at(z)).astype(BF)

    pl.semaphore_wait(barrier, len(near))
    halos[0][0].start()
    halos[0][1].start()
    for dev in x_line + z_near:
        pl.semaphore_signal(round_sem.at[0], inc=1, device_id=dev, device_id_type=MESH)
    halos[1][0].start()
    halos[1][1].start()
    several(up_rows, 0, BS)
    for z in range(GROUP):
        own_plane(z)


    def columns(t):
        return t * PLANE, min(PLANE, TAPS * C - t * PLANE)

    def place(t, n, r):
        if t < 2:
            return slot_of((2 * t + n // 128) * 6 + r), slice(0, 128)
        return slot_of(24 + r // 2), slice(C * (r % 2), C * (r % 2) + C)

    nt = (((1,), (1,)), ((), ()))
    for first in range(0, BS, GROUP):
        lanes = slice((first + 1) * PLANE, (first + 1 + GROUP) * PLANE)
        for t in range(3):
            base, width = columns(t)
            g = lax.dot_general(
                u3[:, lanes], s9f[base : base + width, lanes], nt, preferred_element_type=F32
            )
            if first > 0:
                g += partial[:, base : base + width]
            if first + GROUP < BS:
                partial[:, base : base + width] = g
                continue
            for n in range(0, width, 128):
                w = min(128, width - n)
                for r in range(6):
                    at, cols = place(t, n, r)
                    part[at, :, cols] = g[32 * r : 32 * r + 32, n : n + w]
        for z in range(first + GROUP, min(first + 2 * GROUP, BS)):
            own_plane(z)

    pl.semaphore_wait(round_sem.at[0], len(x_line) + len(z_near))
    for dev in z_next:
        pl.semaphore_signal(round_sem.at[1], inc=1, device_id=dev, device_id_type=MESH)

    halos[0][0].wait_recv()
    halos[0][1].wait_recv()
    for n, layer in ((0, 0), (1, 2)):
        slot = layer * (BS + 1) // 2
        fill(s9f, halo_recv[0, n].astype(F32), layer, slot)
        edge = u3[layer * C : layer * C + C, slot * PLANE : slot * PLANE + PLANE]
        for t in range(3):
            base, width = columns(t)
            g = lax.dot_general(
                edge, s9f[base : base + width, slot * PLANE : slot * PLANE + PLANE], nt,
                preferred_element_type=F32,
            )
            for m in range(0, width, 128):
                w = min(128, width - m)
                for h in range(2):
                    at, cols = place(t, m, 2 * layer + h)
                    part[at, :, cols] += g[32 * h : 32 * h + 32, m : m + w]

    rows = [slice(SUB * s, SUB * s + SUB) for s in range(SUBS)]

    def pair_copy(s):
        return pltpu.make_async_remote_copy(
            src_ref=part.at[pl.ds((1 - cc) * N_XY, OWNERS), rows[s]],
            dst_ref=pair_recv.at[0:OWNERS, rows[s]],
            send_sem=pair_ssem.at[s],
            recv_sem=pair_rsem.at[s],
            device_id=pair_dev,
            device_id_type=MESH,
        )

    pairs = [pair_copy(s) for s in range(SUBS)]
    for copy in pairs:
        copy.start()

    def xy_copy(s, j):
        i, dev = xy_peer(j)
        return pltpu.make_async_remote_copy(
            src_ref=half.at[i, rows[s]],
            dst_ref=xy_recv.at[j, rows[s]],
            send_sem=xy_ssem.at[s, j],
            recv_sem=xy_rsem.at[s, j],
            device_id=dev,
            device_id_type=MESH,
        )

    xy_order = [10, 9, 11, 6, 7, 5, 14, 8, 2, 13, 3, 1, 15, 4, 12]
    xy_copies = []
    for s in range(SUBS):
        pairs[s].wait_recv()
        half[0:OWNERS, rows[s]] = part[pl.ds(cc * N_XY, OWNERS), rows[s]] + pair_recv[0:OWNERS, rows[s]]
        xy_copies.append({j: xy_copy(s, j) for j in xy_order})
        for j in xy_order:
            pl.when(lax.rem(xy + j, N_XY) < OWNERS)(xy_copies[s][j].start)

    w_in.wait()
    for k in range(27):
        dz, j = k // 9, k % 9
        wf[dz * C : (dz + 1) * C, j * C : (j + 1) * C] = w_ref[k]
        wb[dz * C : (dz + 1) * C, j * C : (j + 1) * C] = jnp.transpose(w_ref[26 - k].astype(F32)).astype(BF)

    def convolve(weights, s9, dst):
        step = 6 * PLANE
        for n in range(0, EXT, step):
            products[:, n : n + step] = jnp.dot(
                weights[...], s9[:, n : n + step], preferred_element_type=F32
            )

        def combine(z, carry):
            z0 = pl.multiple_of(z * PLANE, PLANE)
            acc = products[0:C, pl.ds(z0, PLANE)]
            for dz in (1, 2):
                acc += products[dz * C : dz * C + C, pl.ds(pl.multiple_of(z0 + dz * PLANE, PLANE), PLANE)]
            dst[:, pl.ds(z0, PLANE)] = (acc * occ_ref[:, pl.ds(z0, PLANE)].astype(F32)).astype(BF)
            return carry

        lax.fori_loop(0, BS, combine, 0)

    convolve(wf, s9f, out_v)
    out_copy = pltpu.make_async_copy(out_v, out_hbm, out_sem.at[0])
    out_copy.start()

    def up_plane(z):
        z0 = pl.multiple_of((z + 1) * PLANE, PLANE)
        fill(s9u, u3[C : 2 * C, pl.ds(z0, PLANE)].astype(F32), 1, z + 1)

    several(up_plane, 0, UP_SPLIT)

    def z_copy(s, j):
        return pltpu.make_async_remote_copy(
            src_ref=own.at[rows[s]],
            dst_ref=z_recv.at[j, rows[s]],
            send_sem=z_ssem.at[s, j],
            recv_sem=z_rsem.at[s, j],
            device_id=z_peer(j),
            device_id_type=MESH,
        )

    pl.semaphore_wait(round_sem.at[1], len(z_next))
    z_order = [4, 3, 5, 2, 6, 1, 7]
    owner = xy < OWNERS
    z_copies = [{j: z_copy(s, j) for j in z_order} for s in range(SUBS)]

    @pl.when(owner)
    def _():
        for s in range(SUBS):
            acc = half[xy, rows[s]]
            for j in xy_order:
                xy_copies[s][j].wait_recv()
            for j in xy_order:
                acc += xy_recv[j, rows[s]]
            own[rows[s]] = acc
            for copy in z_copies[s].values():
                copy.start()

    halos[1][0].wait_recv()
    halos[1][1].wait_recv()
    fill(s9u, halo_recv[1, 0].astype(F32), 0, 0)
    fill(s9u, halo_recv[1, 1].astype(F32), 2, BS + 1)

    several(up_plane, UP_SPLIT, BS)
    convolve(wb, s9u, gin_v)
    gin_copy = pltpu.make_async_copy(gin_v, gin_hbm, out_sem.at[1])
    gin_copy.start()

    def back_copy(s, j):
        i, dev = xy_peer(j)
        return pltpu.make_async_remote_copy(
            src_ref=total.at[rows[s]],
            dst_ref=final.at[cc * N_XY + xy, rows[s]],
            send_sem=back_ssem.at[s, j],
            recv_sem=back_rsem.at[s, j],
            device_id=dev,
            device_id_type=MESH,
        )

    def forward(s, i):
        slot = final.at[cc * N_XY + i, rows[s]]
        copy = pltpu.make_async_remote_copy(
            src_ref=slot, dst_ref=slot, send_sem=on_ssem.at[s, i], recv_sem=on_rsem.at[s, i],
            device_id=pair_dev, device_id_type=MESH,
        )
        return copy

    back_copies = [{j: back_copy(s, j) for j in xy_order} for s in range(SUBS)]
    forwards = [{j: forward(s, lax.rem(xy + N_XY - j, N_XY)) for j in range(N_XY)} for s in range(SUBS)]

    @pl.when(owner)
    def _():
        for s in range(SUBS):
            for j in z_order:
                z_copies[s][j].wait_recv()
            z_recv[0, rows[s]] = own[rows[s]]
            acc = z_recv[cz, rows[s]]
            for n in range(1, N_Z):
                acc += z_recv[lax.rem(cz + N_Z - n, N_Z), rows[s]]
            total[rows[s]] = acc
            for copy in back_copies[s].values():
                copy.start()
            final[cc * N_XY + xy, rows[s]] = acc
            chunk_ref[cc * N_XY + xy, rows[s]] = acc
            forwards[s][0].start()

    def sender(j):
        return lax.rem(xy + N_XY - j, N_XY)

    def pass_on(s, j):
        back_copies[s][j].wait_recv()
        forwards[s][j].start()
        chunk_ref[cc * N_XY + sender(j), rows[s]] = final[cc * N_XY + sender(j), rows[s]]

    for s in range(SUBS):
        for j in reversed(xy_order):
            pl.when(sender(j) < OWNERS)(functools.partial(pass_on, s, j))
    for s in range(SUBS):
        for j in range(N_XY):
            pl.when(sender(j) < OWNERS)(forwards[s][j].wait_recv)
    other = pl.ds((1 - cc) * N_XY, OWNERS)
    chunk_ref[other] = final[other]

    for s in range(SUBS):
        pairs[s].wait_send()
        for j in xy_order:
            pl.when(lax.rem(xy + j, N_XY) < OWNERS)(xy_copies[s][j].wait_send)
        for j in range(N_XY):
            pl.when(sender(j) < OWNERS)(forwards[s][j].wait_send)

    @pl.when(owner)
    def _():
        for s in range(SUBS):
            for copies in (z_copies[s], back_copies[s]):
                for copy in copies.values():
                    copy.wait_send()

    for field in range(2):
        for n in range(2):
            halos[field][n].wait_send()
    out_copy.wait()
    gin_copy.wait()


def deliver(out_ref, gin_ref, chunk_ref, out_hbm, gin_hbm, gw_hbm, gw_v, sems):
    copies = [
        pltpu.make_async_copy(out_ref, out_hbm, sems.at[0]),
        pltpu.make_async_copy(gin_ref, gin_hbm, sems.at[1]),
    ]
    for copy in copies:
        copy.start()
    for k in range(27):
        dz, j = k // 9, k % 9
        for h in range(2):
            if j < 8:
                at, half = slot_of((j // 2) * 6 + 2 * dz + h), j % 2
            else:
                at, half = slot_of(24 + dz), h
            gw_v[k, 32 * h : 32 * h + 32, :] = chunk_ref[at, :, C * half : C * half + C]
    gw_copy = pltpu.make_async_copy(gw_v, gw_hbm, sems.at[2])
    gw_copy.start()
    for copy in copies:
        copy.wait()
    gw_copy.wait()


def local(features, cotangent, weight, neighbours, occupancy):
    hbm = pl.BlockSpec(memory_space=pltpu.HBM)
    vmem = pl.BlockSpec(memory_space=pltpu.VMEM)
    anywhere = pl.BlockSpec(memory_space=pl.ANY)
    field = jax.ShapeDtypeStruct((C, V), BF)
    output, grad_input, chunks = pl.pallas_call(
        kernel,
        out_shape=(field, field, jax.ShapeDtypeStruct((32, 32, 128), F32)),
        in_specs=[hbm, hbm, hbm, hbm, hbm],
        out_specs=(anywhere, anywhere, vmem),
        scratch_shapes=[
            pltpu.VMEM((C, V), BF),
            pltpu.VMEM((C, V), BF),
            pltpu.VMEM((2, C, PLANE), BF),
            pltpu.VMEM((27, C, C), BF),
            pltpu.SMEM((1, 27), jnp.int32),
            pltpu.VMEM((1, V), jnp.int32),
            pltpu.VMEM((C, V), BF),
            pltpu.VMEM((C, V), BF),
            pltpu.VMEM((3 * C, EXT), F32),
            pltpu.VMEM((3 * C, TAPS * C), F32),
            pltpu.VMEM((3, TAPS, C, PLANE), BF),
            pltpu.VMEM((TAPS * C, EXT), BF),
            pltpu.VMEM((TAPS * C, EXT), BF),
            pltpu.VMEM((3 * C, EXT), BF),
            pltpu.VMEM((3 * C, TAPS * C), BF),
            pltpu.VMEM((3 * C, TAPS * C), BF),
            pltpu.VMEM((2, 2, C, PLANE), BF),
            pltpu.VMEM((2, 2, C, PLANE), BF),
            pltpu.VMEM((32, 32, 128), F32),
            pltpu.VMEM((16, 32, 128), F32),
            pltpu.VMEM((16, 32, 128), F32),
            pltpu.VMEM((16, 32, 128), F32),
            pltpu.VMEM((32, 128), F32),
            pltpu.VMEM((8, 32, 128), F32),
            pltpu.VMEM((32, 128), F32),
            pltpu.VMEM((32, 32, 128), F32),
            pltpu.SemaphoreType.DMA((7,)),
            pltpu.SemaphoreType.DMA((3,)),
            pltpu.SemaphoreType.DMA((2, 2)),
            pltpu.SemaphoreType.DMA((2, 2)),
            pltpu.SemaphoreType.DMA((SUBS,)),
            pltpu.SemaphoreType.DMA((SUBS,)),
            pltpu.SemaphoreType.DMA((SUBS, N_XY)),
            pltpu.SemaphoreType.DMA((SUBS, N_XY)),
            pltpu.SemaphoreType.DMA((SUBS, N_Z)),
            pltpu.SemaphoreType.DMA((SUBS, N_Z)),
            pltpu.SemaphoreType.DMA((SUBS, N_XY)),
            pltpu.SemaphoreType.DMA((SUBS, N_XY)),
            pltpu.SemaphoreType.DMA((SUBS, N_XY)),
            pltpu.SemaphoreType.DMA((SUBS, N_XY)),
            pltpu.SemaphoreType.REGULAR((2,)),
        ],
        compiler_params=pltpu.CompilerParams(
            collective_id=0, has_side_effects=True, vmem_limit_bytes=40 * 2**20
        ),
    )(
        pltpu.with_memory_space_constraint(features.reshape(C, V), pltpu.HBM),
        pltpu.with_memory_space_constraint(cotangent.reshape(C, V), pltpu.HBM),
        pltpu.with_memory_space_constraint(weight, pltpu.HBM),
        pltpu.with_memory_space_constraint(neighbours.reshape(1, 27), pltpu.HBM),
        pltpu.with_memory_space_constraint(occupancy.reshape(1, V), pltpu.HBM),
    )
    output, grad_input, grad_weight = pl.pallas_call(
        deliver,
        out_shape=(field, field, jax.ShapeDtypeStruct((27, C, C), F32)),
        in_specs=[anywhere, anywhere, vmem],
        out_specs=(hbm, hbm, hbm),
        scratch_shapes=[
            pltpu.VMEM((27, C, C), F32),
            pltpu.SemaphoreType.DMA((3,)),
        ],
        compiler_params=pltpu.CompilerParams(vmem_limit_bytes=16 * 2**20),
    )(output, grad_input, chunks)
    return output.reshape(1, 1, C, V), grad_input.reshape(1, 1, C, V), grad_weight


def solution(mesh):
    in_specs = (
        P("scan", "brick", None, None),
        P("scan", "brick", None, None),
        P(),
        P("scan", "brick", None),
        P("scan", "brick", None),
    )
    out_specs = (P("scan", "brick", None, None), P("scan", "brick", None, None), P())
    return jax.shard_map(local, mesh=mesh, in_specs=in_specs, out_specs=out_specs, check_vma=False)
```

```python
import functools

import jax
import jax.numpy as jnp
from jax import lax
from jax.experimental import pallas as pl
from jax.experimental.pallas import tpu as pltpu
from jax.sharding import PartitionSpec as P

C = 64
BS = 16
PLANE = BS * BS
V = BS * PLANE
EXT = (BS + 2) * PLANE
TAPS = 9
BF = jnp.bfloat16
F32 = jnp.float32
MESH = pl.DeviceIdType.MESH
N_CORE, N_X, N_Y, N_Z = 2, 4, 4, 8
N_BRICK = N_Y * N_Z
N_XY = N_X * N_Y
UNROLL = 4
SUBS = 1
SUB = 32 // SUBS
UP_SPLIT = 16
GROUP = 2


OWNERS = 14


def slot_of(chunk):
    return chunk if chunk < OWNERS else chunk - OWNERS + N_XY


def spread(plane, x_iota):
    left = jnp.where(x_iota == 0, pltpu.roll(plane, PLANE - 15, 1), pltpu.roll(plane, 1, 1))
    right = jnp.where(x_iota == BS - 1, pltpu.roll(plane, 15, 1), pltpu.roll(plane, PLANE - 1, 1))
    shifted = []
    for dy in (-1, 0, 1):
        for base in (left, plane, right):
            shifted.append(base if dy == 0 else pltpu.roll(base, (-dy * BS) % PLANE, 1))
    return shifted


def kernel(
    feat_hbm, cot_hbm, w_hbm, nb_hbm, occ_hbm,
    out_hbm, gin_hbm, chunk_ref,
    feat_v, cot_v, edge_v, w_ref, nb_ref, occ_ref, out_v, gin_v, products, partial, mask_v, s9f, s9u, u3, wf, wb,
    halo_send, halo_recv, part, pair_recv, half, xy_recv, own, z_recv, total, final,
    in_sem, out_sem, halo_ssem, halo_rsem, pair_ssem, pair_rsem, xy_ssem, xy_rsem, z_ssem, z_rsem, back_ssem, back_rsem, on_ssem, on_rsem, round_sem,
):
    scan = lax.axis_index("scan")
    brick = lax.axis_index("brick")
    cx, cc = scan // N_CORE, scan % N_CORE
    cz, cy = brick // N_Y, brick % N_Y
    xy = cx * N_Y + cy
    up_dev = (scan, lax.rem(brick + 1, N_BRICK))
    down_dev = (scan, lax.rem(brick + N_BRICK - 1, N_BRICK))
    pair_dev = (cx * N_CORE + 1 - cc, brick)

    def xy_peer(j):
        i = lax.rem(xy + j, N_XY)
        return i, ((i // N_Y) * N_CORE + cc, cz * N_Y + lax.rem(i, N_Y))

    def z_peer(j):
        return (scan, lax.rem(cz + j, N_Z) * N_Y + cy)

    def edge_in(hbm, n):
        lanes = pl.ds((BS - 1) * PLANE * (1 - n), PLANE)
        return pltpu.make_async_copy(hbm.at[:, lanes], edge_v.at[n], in_sem.at[5 + n])

    edges = [edge_in(feat_hbm, n) for n in range(2)]
    feat_in = pltpu.make_async_copy(feat_hbm, feat_v, in_sem.at[0])
    cot_in = pltpu.make_async_copy(cot_hbm, cot_v, in_sem.at[1])
    w_in = pltpu.make_async_copy(w_hbm, w_ref, in_sem.at[2])
    occ_in = pltpu.make_async_copy(occ_hbm, occ_ref, in_sem.at[3])
    nb_in = pltpu.make_async_copy(nb_hbm, nb_ref, in_sem.at[4])
    occ_in.start()
    edges[0].start()
    edges[1].start()

    cot_in.start()
    w_in.start()
    nb_in.start()

    def around(dx, dy, dz):
        return (
            lax.rem(cx + dx, N_X) * N_CORE + cc,
            lax.rem(cz + dz, N_Z) * N_Y + lax.rem(cy + dy, N_Y),
        )

    x_line = [around(dx, 0, 0) for dx in (2, 1, 3)]
    y_line = [around(0, dy, 0) for dy in (2, 1, 3)]
    z_near = [around(0, 0, 1), around(0, 0, N_Z - 1)]
    z_next = [around(0, 0, 2), around(0, 0, N_Z - 2)]

    barrier = pltpu.get_barrier_semaphore()
    near = [up_dev, down_dev, pair_dev] + x_line + y_line + z_near
    for dev in near:
        pl.semaphore_signal(barrier, inc=1, device_id=dev, device_id_type=MESH)
    feat_in.start()
    def occ_at(z):
        return occ_ref[:, pl.ds(z * PLANE, PLANE)].astype(F32)

    occ_in.wait()
    for n, z in enumerate((BS - 1, 0)):
        edges[n].wait()
        halo_send[0, n] = (edge_v[n].astype(F32) * occ_at(z)).astype(BF)

    def halo_copy(field, n):
        return pltpu.make_async_remote_copy(
            src_ref=halo_send.at[field, n],
            dst_ref=halo_recv.at[field, n],
            send_sem=halo_ssem.at[field, n],
            recv_sem=halo_rsem.at[field, n],
            device_id=(up_dev, down_dev)[n],
            device_id_type=MESH,
        )

    halos = [[halo_copy(field, n) for n in range(2)] for field in range(2)]
    def lane_of(plane):
        return plane * PLANE if isinstance(plane, int) else pl.multiple_of(plane * PLANE, PLANE)

    def fill(s9, plane, layer, slot):
        lanes = pl.ds(lane_of(slot), PLANE)
        for k, moved in enumerate(spread(plane, x_iota)):
            s9[k * C : (k + 1) * C, lanes] = moved.astype(BF) * mask_v[layer, k]

    nb_in.wait()
    lane = lax.broadcasted_iota(jnp.int32, (C, PLANE), 1)
    x_iota = lane % BS
    y_iota = lane // BS
    for layer in range(3):
        flag = [jnp.where(nb_ref[0, 9 * layer + k] >= 0, 1.0, 0.0).astype(F32) for k in range(9)]
        for dy in (-1, 0, 1):
            y_out = y_iota == (BS - 1 if dy == 1 else 0 if dy == -1 else -1)
            for dx in (-1, 0, 1):
                x_out = x_iota == (BS - 1 if dx == 1 else 0 if dx == -1 else -1)

                def at(a, b):
                    return flag[3 * (a + 1) + b + 1]

                inner = jnp.where(x_out, at(0, dx), at(0, 0))
                outer = jnp.where(x_out, at(dy, dx), at(dy, 0))
                mask_v[layer, 3 * (dy + 1) + dx + 1] = jnp.where(y_out, outer, inner).astype(BF)


    def several(body, first, last):
        def step(n, carry):
            for m in range(UNROLL):
                body(first + n * UNROLL + m)
            return carry

        lax.fori_loop(0, (last - first) // UNROLL, step, 0)

    def own_plane(z):
        z0 = lane_of(z)
        occ = occ_ref[:, pl.ds(z0, PLANE)].astype(F32)
        fill(s9f, feat_v[:, pl.ds(z0, PLANE)].astype(F32) * occ, 1, z + 1)

    def up_rows(z):
        z0 = lane_of(z)
        occ = occ_ref[:, pl.ds(z0, PLANE)].astype(F32)
        ups = (cot_v[:, pl.ds(z0, PLANE)].astype(F32) * occ).astype(BF)
        for dz in range(3):
            u3[dz * C : (dz + 1) * C, pl.ds(lane_of(z + dz), PLANE)] = ups

    for n in (14, 15, 29, 30, 31):
        part[n] = jnp.zeros((32, 128), F32)
    u3[0:C, V : V + PLANE] = jnp.zeros((C, PLANE), BF)
    u3[2 * C : 3 * C, PLANE : 2 * PLANE] = jnp.zeros((C, PLANE), BF)
    pl.semaphore_wait(barrier, len(near))
    halos[0][0].start()
    halos[0][1].start()
    for dev in x_line + z_near:
        pl.semaphore_signal(round_sem.at[0], inc=1, device_id=dev, device_id_type=MESH)
    feat_in.wait()
    cot_in.wait()
    for n, z in enumerate((BS - 1, 0)):
        halo_send[1, n] = (cot_v[:, z * PLANE : (z + 1) * PLANE].astype(F32) * occ_at(z)).astype(BF)
    halos[1][0].start()
    halos[1][1].start()
    several(up_rows, 0, BS)
    for z in range(GROUP):
        own_plane(z)


    def columns(t):
        return t * PLANE, min(PLANE, TAPS * C - t * PLANE)

    def place(t, n, r):
        if t < 2:
            return slot_of((2 * t + n // 128) * 6 + r), slice(0, 128)
        return slot_of(24 + r // 2), slice(C * (r % 2), C * (r % 2) + C)

    nt = (((1,), (1,)), ((), ()))
    for first in range(0, BS, GROUP):
        lanes = slice((first + 1) * PLANE, (first + 1 + GROUP) * PLANE)
        for t in range(3):
            base, width = columns(t)
            g = lax.dot_general(
                u3[:, lanes], s9f[base : base + width, lanes], nt, preferred_element_type=F32
            )
            if first > 0:
                g += partial[:, base : base + width]
            if first + GROUP < BS:
                partial[:, base : base + width] = g
                continue
            for n in range(0, width, 128):
                w = min(128, width - n)
                for r in range(6):
                    at, cols = place(t, n, r)
                    part[at, :, cols] = g[32 * r : 32 * r + 32, n : n + w]
        for z in range(first + GROUP, min(first + 2 * GROUP, BS)):
            own_plane(z)

    pl.semaphore_wait(round_sem.at[0], len(x_line) + len(z_near))
    for dev in z_next:
        pl.semaphore_signal(round_sem.at[1], inc=1, device_id=dev, device_id_type=MESH)

    halos[0][0].wait_recv()
    halos[0][1].wait_recv()
    for n, layer in ((0, 0), (1, 2)):
        slot = layer * (BS + 1) // 2
        fill(s9f, halo_recv[0, n].astype(F32), layer, slot)
        edge = u3[layer * C : layer * C + C, slot * PLANE : slot * PLANE + PLANE]
        for t in range(3):
            base, width = columns(t)
            g = lax.dot_general(
                edge, s9f[base : base + width, slot * PLANE : slot * PLANE + PLANE], nt,
                preferred_element_type=F32,
            )
            for m in range(0, width, 128):
                w = min(128, width - m)
                for h in range(2):
                    at, cols = place(t, m, 2 * layer + h)
                    part[at, :, cols] += g[32 * h : 32 * h + 32, m : m + w]

    rows = [slice(SUB * s, SUB * s + SUB) for s in range(SUBS)]

    def pair_copy(s):
        return pltpu.make_async_remote_copy(
            src_ref=part.at[pl.ds((1 - cc) * N_XY, OWNERS), rows[s]],
            dst_ref=pair_recv.at[0:OWNERS, rows[s]],
            send_sem=pair_ssem.at[s],
            recv_sem=pair_rsem.at[s],
            device_id=pair_dev,
            device_id_type=MESH,
        )

    pairs = [pair_copy(s) for s in range(SUBS)]
    for copy in pairs:
        copy.start()

    def xy_copy(s, j):
        i, dev = xy_peer(j)
        return pltpu.make_async_remote_copy(
            src_ref=half.at[i, rows[s]],
            dst_ref=xy_recv.at[j, rows[s]],
            send_sem=xy_ssem.at[s, j],
            recv_sem=xy_rsem.at[s, j],
            device_id=dev,
            device_id_type=MESH,
        )

    xy_order = [10, 9, 11, 6, 7, 5, 14, 8, 2, 13, 3, 1, 15, 4, 12]
    xy_copies = []
    for s in range(SUBS):
        pairs[s].wait_recv()
        half[0:OWNERS, rows[s]] = part[pl.ds(cc * N_XY, OWNERS), rows[s]] + pair_recv[0:OWNERS, rows[s]]
        xy_copies.append({j: xy_copy(s, j) for j in xy_order})
        for j in xy_order:
            pl.when(lax.rem(xy + j, N_XY) < OWNERS)(xy_copies[s][j].start)

    w_in.wait()
    for k in range(27):
        dz, j = k // 9, k % 9
        wf[dz * C : (dz + 1) * C, j * C : (j + 1) * C] = w_ref[k]
        wb[dz * C : (dz + 1) * C, j * C : (j + 1) * C] = jnp.transpose(w_ref[26 - k].astype(F32)).astype(BF)

    def convolve(weights, s9, dst):
        step = 6 * PLANE
        for n in range(0, EXT, step):
            products[:, n : n + step] = jnp.dot(
                weights[...], s9[:, n : n + step], preferred_element_type=F32
            )

        def combine(z, carry):
            z0 = pl.multiple_of(z * PLANE, PLANE)
            acc = products[0:C, pl.ds(z0, PLANE)]
            for dz in (1, 2):
                acc += products[dz * C : dz * C + C, pl.ds(pl.multiple_of(z0 + dz * PLANE, PLANE), PLANE)]
            dst[:, pl.ds(z0, PLANE)] = (acc * occ_ref[:, pl.ds(z0, PLANE)].astype(F32)).astype(BF)
            return carry

        lax.fori_loop(0, BS, combine, 0)

    convolve(wf, s9f, out_v)
    out_copy = pltpu.make_async_copy(out_v, out_hbm, out_sem.at[0])
    out_copy.start()

    def up_plane(z):
        z0 = pl.multiple_of((z + 1) * PLANE, PLANE)
        fill(s9u, u3[C : 2 * C, pl.ds(z0, PLANE)].astype(F32), 1, z + 1)

    several(up_plane, 0, UP_SPLIT)

    def z_copy(s, j):
        return pltpu.make_async_remote_copy(
            src_ref=own.at[rows[s]],
            dst_ref=z_recv.at[j, rows[s]],
            send_sem=z_ssem.at[s, j],
            recv_sem=z_rsem.at[s, j],
            device_id=z_peer(j),
            device_id_type=MESH,
        )

    pl.semaphore_wait(round_sem.at[1], len(z_next))
    z_order = [4, 3, 5, 2, 6, 1, 7]
    owner = xy < OWNERS
    z_copies = [{j: z_copy(s, j) for j in z_order} for s in range(SUBS)]

    @pl.when(owner)
    def _():
        for s in range(SUBS):
            acc = half[xy, rows[s]]
            for j in xy_order:
                xy_copies[s][j].wait_recv()
            for j in xy_order:
                acc += xy_recv[j, rows[s]]
            own[rows[s]] = acc
            for copy in z_copies[s].values():
                copy.start()

    halos[1][0].wait_recv()
    halos[1][1].wait_recv()
    fill(s9u, halo_recv[1, 0].astype(F32), 0, 0)
    fill(s9u, halo_recv[1, 1].astype(F32), 2, BS + 1)

    several(up_plane, UP_SPLIT, BS)
    convolve(wb, s9u, gin_v)
    gin_copy = pltpu.make_async_copy(gin_v, gin_hbm, out_sem.at[1])
    gin_copy.start()

    def back_copy(s, j):
        i, dev = xy_peer(j)
        return pltpu.make_async_remote_copy(
            src_ref=total.at[rows[s]],
            dst_ref=final.at[cc * N_XY + xy, rows[s]],
            send_sem=back_ssem.at[s, j],
            recv_sem=back_rsem.at[s, j],
            device_id=dev,
            device_id_type=MESH,
        )

    def forward(s, i):
        slot = final.at[cc * N_XY + i, rows[s]]
        copy = pltpu.make_async_remote_copy(
            src_ref=slot, dst_ref=slot, send_sem=on_ssem.at[s, i], recv_sem=on_rsem.at[s, i],
            device_id=pair_dev, device_id_type=MESH,
        )
        return copy

    back_copies = [{j: back_copy(s, j) for j in xy_order} for s in range(SUBS)]
    forwards = [{j: forward(s, lax.rem(xy + N_XY - j, N_XY)) for j in range(N_XY)} for s in range(SUBS)]

    @pl.when(owner)
    def _():
        for s in range(SUBS):
            for j in z_order:
                z_copies[s][j].wait_recv()
            z_recv[0, rows[s]] = own[rows[s]]
            acc = z_recv[cz, rows[s]]
            for n in range(1, N_Z):
                acc += z_recv[lax.rem(cz + N_Z - n, N_Z), rows[s]]
            total[rows[s]] = acc
            for copy in back_copies[s].values():
                copy.start()
            final[cc * N_XY + xy, rows[s]] = acc
            chunk_ref[cc * N_XY + xy, rows[s]] = acc
            forwards[s][0].start()

    def sender(j):
        return lax.rem(xy + N_XY - j, N_XY)

    def pass_on(s, j):
        back_copies[s][j].wait_recv()
        forwards[s][j].start()
        chunk_ref[cc * N_XY + sender(j), rows[s]] = final[cc * N_XY + sender(j), rows[s]]

    for s in range(SUBS):
        for j in reversed(xy_order):
            pl.when(sender(j) < OWNERS)(functools.partial(pass_on, s, j))
    for s in range(SUBS):
        for j in range(N_XY):
            pl.when(sender(j) < OWNERS)(forwards[s][j].wait_recv)
    other = pl.ds((1 - cc) * N_XY, OWNERS)
    chunk_ref[other] = final[other]

    for s in range(SUBS):
        pairs[s].wait_send()
        for j in xy_order:
            pl.when(lax.rem(xy + j, N_XY) < OWNERS)(xy_copies[s][j].wait_send)
        for j in range(N_XY):
            pl.when(sender(j) < OWNERS)(forwards[s][j].wait_send)

    @pl.when(owner)
    def _():
        for s in range(SUBS):
            for copies in (z_copies[s], back_copies[s]):
                for copy in copies.values():
                    copy.wait_send()

    for field in range(2):
        for n in range(2):
            halos[field][n].wait_send()
    out_copy.wait()
    gin_copy.wait()


def deliver(out_ref, gin_ref, chunk_ref, out_hbm, gin_hbm, gw_hbm, gw_v, sems):
    copies = [
        pltpu.make_async_copy(out_ref, out_hbm, sems.at[0]),
        pltpu.make_async_copy(gin_ref, gin_hbm, sems.at[1]),
    ]
    for copy in copies:
        copy.start()
    for k in range(27):
        dz, j = k // 9, k % 9
        for h in range(2):
            if j < 8:
                at, half = slot_of((j // 2) * 6 + 2 * dz + h), j % 2
            else:
                at, half = slot_of(24 + dz), h
            gw_v[k, 32 * h : 32 * h + 32, :] = chunk_ref[at, :, C * half : C * half + C]
    gw_copy = pltpu.make_async_copy(gw_v, gw_hbm, sems.at[2])
    gw_copy.start()
    for copy in copies:
        copy.wait()
    gw_copy.wait()


def local(features, cotangent, weight, neighbours, occupancy):
    hbm = pl.BlockSpec(memory_space=pltpu.HBM)
    vmem = pl.BlockSpec(memory_space=pltpu.VMEM)
    anywhere = pl.BlockSpec(memory_space=pl.ANY)
    field = jax.ShapeDtypeStruct((C, V), BF)
    output, grad_input, chunks = pl.pallas_call(
        kernel,
        out_shape=(field, field, jax.ShapeDtypeStruct((32, 32, 128), F32)),
        in_specs=[hbm, hbm, hbm, hbm, hbm],
        out_specs=(anywhere, anywhere, vmem),
        scratch_shapes=[
            pltpu.VMEM((C, V), BF),
            pltpu.VMEM((C, V), BF),
            pltpu.VMEM((2, C, PLANE), BF),
            pltpu.VMEM((27, C, C), BF),
            pltpu.SMEM((1, 27), jnp.int32),
            pltpu.VMEM((1, V), jnp.int32),
            pltpu.VMEM((C, V), BF),
            pltpu.VMEM((C, V), BF),
            pltpu.VMEM((3 * C, EXT), F32),
            pltpu.VMEM((3 * C, TAPS * C), F32),
            pltpu.VMEM((3, TAPS, C, PLANE), BF),
            pltpu.VMEM((TAPS * C, EXT), BF),
            pltpu.VMEM((TAPS * C, EXT), BF),
            pltpu.VMEM((3 * C, EXT), BF),
            pltpu.VMEM((3 * C, TAPS * C), BF),
            pltpu.VMEM((3 * C, TAPS * C), BF),
            pltpu.VMEM((2, 2, C, PLANE), BF),
            pltpu.VMEM((2, 2, C, PLANE), BF),
            pltpu.VMEM((32, 32, 128), F32),
            pltpu.VMEM((16, 32, 128), F32),
            pltpu.VMEM((16, 32, 128), F32),
            pltpu.VMEM((16, 32, 128), F32),
            pltpu.VMEM((32, 128), F32),
            pltpu.VMEM((8, 32, 128), F32),
            pltpu.VMEM((32, 128), F32),
            pltpu.VMEM((32, 32, 128), F32),
            pltpu.SemaphoreType.DMA((7,)),
            pltpu.SemaphoreType.DMA((3,)),
            pltpu.SemaphoreType.DMA((2, 2)),
            pltpu.SemaphoreType.DMA((2, 2)),
            pltpu.SemaphoreType.DMA((SUBS,)),
            pltpu.SemaphoreType.DMA((SUBS,)),
            pltpu.SemaphoreType.DMA((SUBS, N_XY)),
            pltpu.SemaphoreType.DMA((SUBS, N_XY)),
            pltpu.SemaphoreType.DMA((SUBS, N_Z)),
            pltpu.SemaphoreType.DMA((SUBS, N_Z)),
            pltpu.SemaphoreType.DMA((SUBS, N_XY)),
            pltpu.SemaphoreType.DMA((SUBS, N_XY)),
            pltpu.SemaphoreType.DMA((SUBS, N_XY)),
            pltpu.SemaphoreType.DMA((SUBS, N_XY)),
            pltpu.SemaphoreType.REGULAR((2,)),
        ],
        compiler_params=pltpu.CompilerParams(
            collective_id=0, has_side_effects=True, vmem_limit_bytes=40 * 2**20
        ),
    )(
        pltpu.with_memory_space_constraint(features.reshape(C, V), pltpu.HBM),
        pltpu.with_memory_space_constraint(cotangent.reshape(C, V), pltpu.HBM),
        pltpu.with_memory_space_constraint(weight, pltpu.HBM),
        pltpu.with_memory_space_constraint(neighbours.reshape(1, 27), pltpu.HBM),
        pltpu.with_memory_space_constraint(occupancy.reshape(1, V), pltpu.HBM),
    )
    output, grad_input, grad_weight = pl.pallas_call(
        deliver,
        out_shape=(field, field, jax.ShapeDtypeStruct((27, C, C), F32)),
        in_specs=[anywhere, anywhere, vmem],
        out_specs=(hbm, hbm, hbm),
        scratch_shapes=[
            pltpu.VMEM((27, C, C), F32),
            pltpu.SemaphoreType.DMA((3,)),
        ],
        compiler_params=pltpu.CompilerParams(vmem_limit_bytes=16 * 2**20),
    )(output, grad_input, chunks)
    return output.reshape(1, 1, C, V), grad_input.reshape(1, 1, C, V), grad_weight


def solution(mesh):
    in_specs = (
        P("scan", "brick", None, None),
        P("scan", "brick", None, None),
        P(),
        P("scan", "brick", None),
        P("scan", "brick", None),
    )
    out_specs = (P("scan", "brick", None, None), P("scan", "brick", None, None), P())
    return jax.shard_map(local, mesh=mesh, in_specs=in_specs, out_specs=out_specs, check_vma=False)
```
